128 devices in a mesh: grp: 4 (over y), dev: 32 (over x, z, core).
Axes of the slice: x: 4, y: 4, z: 4, core: 2. Of those that a mesh axis runs over, the one named last changes fastest.
Arguments:
- panel_nodes: float32 [3, 1048576], P(None, ('grp', 'dev')), may hold values from -1.6 to 1.6, as said below
- density: float32 [1048576], P(('grp', 'dev')), may hold values from -6 to 6
- crevice_routes: int32 [65536, 2], P(('grp', 'dev')), may hold values from 0 to 127, all different within a row; in each aligned block of 512 rows (0 to 511, 512 to 1023, ...) at most 16 rows name the same one
- crevice_centre: int32 [65536, 2], P(('grp', 'dev')), may hold values from 0 to 511
- centres: float32 [3, 65536], P(None, ('grp', 'dev')), may hold values from -0.3 to 0.3, as said below
- targets: float32 [3, 1048576], P(None, ('grp', 'dev')), may hold values from -0.8 to 0.8, as said below
- centre_home: int32 [65536, 1], P(('grp', 'dev')), may hold values from 0 to 127; in each aligned block of 512 rows (0 to 511, 512 to 1023, ...) at most 8 rows name the same one
- upsample: float32 [64, 16], replicated, may hold values from 0 to 1, as said below
- fine_weights: float32 [64], replicated, may hold values from 0.005 to 0.05
Outputs:
- returned: float32 [2097152], P(('grp', 'dev'))
The draws below stay inside these ranges and needn't reach their ends.
Inputs may be any that keep to these rules, and one draw needn't show every extreme that they name: `crevice_routes`: each device's 512 panels name at most 16 (panel, route) pairs for any one owner device, and some owner reaches 16 in every draw; the 2 owners of one panel differ. `centre_home`: among the 512 centres of one device at most 8 have the same home, and that bound is reached in every draw; entries of returned with no centre are zero. `panel_nodes`: every point in the convex hull of one panel's nodes lies at distance 0.9 or more from the anchor; every panel node lies within 1.6 of the anchor. `centres`: every centre lies within 0.3 of the anchor. `targets`: each target node lies at distance 0.3 to 0.5 from its centre. `upsample`: entries are positive and each row sums to one.
All inputs are finite; a program needn't handle non-finite values.
Results may differ from the reference program's by a relative error of at most 0.0003.
Values sent between devices are 32-bit elements; how exact they have to be, the bound alone decides.
A program may use at most 64 MiB of HBM per device.

```python
import math
import jax
import jax.numpy as jnp
import numpy as np
from jax import lax

NODES = 16
FINE = 64
ORDER = 8
TOP = 2
P_DEV = 512
C_DEV = 512
PANELS = 65536
CENTRES = 65536
MOST = 16
MOST_BACK = 8
DEVICES = 128


def centre_positions(key):
    return jax.random.uniform(jax.random.fold_in(key, 11), (3, CENTRES), jnp.float32, -0.17, 0.17)


def directions(key, count):
    first, second = jax.random.split(key)
    height = jax.random.uniform(first, (count,), jnp.float32, -1.0, 1.0)
    angle = jax.random.uniform(second, (count,), jnp.float32, -3.14159265, 3.14159265)
    across = jnp.sqrt(1.0 - height * height)
    return jnp.stack([across * jnp.cos(angle), across * jnp.sin(angle), height])


def surface_frame(key, count):
    first, second = jax.random.split(key)
    height = jax.random.uniform(first, (count,), jnp.float32, -1.0, 1.0)
    angle = jax.random.uniform(second, (count,), jnp.float32, -3.14159265, 3.14159265)
    across = jnp.sqrt(1.0 - height * height)
    outward = jnp.stack([across * jnp.cos(angle), across * jnp.sin(angle), height])
    first_side = jnp.stack([-jnp.sin(angle), jnp.cos(angle), jnp.zeros_like(angle)])
    second_side = jnp.stack([height * jnp.cos(angle), height * jnp.sin(angle), -across])
    return (outward, first_side, second_side)


def draw_panel_nodes(key, part):
    first, second, third, fourth = jax.random.split(key, 4)
    radius = jax.random.uniform(first, (PANELS,), jnp.float32, 0.9, 1.2)
    along = jax.random.uniform(third, (2, PANELS, NODES), jnp.float32, -0.7, 0.7)
    lift = jax.random.uniform(fourth, (PANELS, NODES), jnp.float32, 0.0, 0.05)
    outward, first_side, second_side = surface_frame(second, PANELS)
    height = radius[:, None] + lift
    nodes = outward[:, :, None] * height[None, :, :] + first_side[:, :, None] * along[0][None, :, :] + second_side[:, :, None] * along[1][None, :, :]
    return nodes.reshape(3, PANELS * NODES).astype(jnp.float32)


def draw_centres(key, part):
    return centre_positions(key)


def draw_targets(key, part):
    middle = centre_positions(key)
    first, second = jax.random.split(jax.random.fold_in(key, 23))
    radius = jax.random.uniform(first, (CENTRES * NODES,), jnp.float32, 0.3, 0.5)
    offset = directions(second, CENTRES * NODES) * radius[None, :]
    return (jnp.repeat(middle, NODES, axis=1) + offset).astype(jnp.float32)


def draw_upsample(key, part):
    first, second = jax.random.split(jax.random.fold_in(key, 31))
    base = 0.1 * jax.random.uniform(first, (FINE, NODES), jnp.float32, 0.05, 1.0) ** 6
    peak = jax.random.uniform(second, (FINE, 1), jnp.float32, 0.6, 1.0)
    nearest = (jnp.arange(FINE, dtype=jnp.int32) % NODES)[:, None] == jnp.arange(NODES, dtype=jnp.int32)[None, :]
    raw = base + jnp.where(nearest, peak, 0.0)
    return (raw / jnp.sum(raw, axis=1, keepdims=True)).astype(jnp.float32)


def place_ends(result, stream_key, low, largest):
    longest = result.shape.index(max(result.shape))
    spots = []
    for shift in (0, 1):
        where = [jax.random.randint(jax.random.fold_in(stream_key, axis), (), 0, length) for axis, length in enumerate(result.shape)]
        where[longest] = (where[longest] + shift) % result.shape[longest]
        spots.append(tuple(where))
    return result.at[spots[0]].set(low).at[spots[1]].set(largest)


def steps_of(stream_key, shape, cuts, least, top_value):
    gain = 1.0
    for axis_at, shards_of in cuts:
        heights = jax.random.uniform(jax.random.fold_in(jax.random.fold_in(stream_key, 6), axis_at), (shards_of,), jnp.float32, least / len(cuts), top_value / len(cuts))
        gain = gain * jnp.repeat(jnp.exp(heights), shape[axis_at] // shards_of).reshape((-1,) + (1,) * (len(shape) - 1 - axis_at))
    return gain


def assign_block(stream_key, own, number, rows, count, top, reach, lean):
    sequence = jax.random.permutation(stream_key, count)
    packed, usual = shares(count, rows * top, reach, lean, True), shares(count, rows * top, reach, lean, False)
    places = jnp.arange(count)

    def named(lengths, offset_by):
        used = int((lengths > 0).sum())
        fixed = max(1, used // 4)
        passed = fixed + (places - fixed + offset_by * (used - fixed)) % max(1, count - fixed)
        return jnp.zeros((count,), jnp.int32).at[sequence[jnp.where(places < fixed, places, passed)]].set(jnp.asarray(lengths, jnp.int32))

    lengths = jnp.where(number % 4 == 0, named(packed, number // 4), named(usual, number - number // 4 - 1))
    mixed = jax.random.permutation(jax.random.fold_in(own, 3), count)
    source_of, taker = mixed[0:count // 2 * 2:2], mixed[1:count // 2 * 2:2]
    slack = jnp.minimum(lengths[source_of] - 1, reach - lengths[taker]) // 2
    slack = jnp.where((source_of == sequence[0]) | (taker == sequence[0]) | (lengths[taker] == 0), 0, jnp.maximum(slack, 0))
    passed = jax.random.randint(jax.random.fold_in(own, 4), (count // 2,), 0, 1 << 20) % (slack + 1)
    lengths = lengths.at[source_of].add(-passed).at[taker].add(passed)
    members = jnp.searchsorted(jnp.cumsum(lengths), jnp.arange(rows * top), side="right").astype(jnp.int32)
    grid = members.reshape(top, rows).T
    grid = grid[jax.random.permutation(jax.random.fold_in(own, 1), rows)]
    offset_by = jax.random.randint(jax.random.fold_in(own, 2), (rows, 1), 0, top)
    return jnp.take_along_axis(grid, (jnp.arange(top)[None, :] + offset_by) % top, axis=1)


def shares(amount, total, reach, lean, full):
    weights = [(1 << 20) // math.isqrt(rank ** lean) + 1 for rank in range(1, amount + 1)]
    largest = reach if full else min(reach, max(-(-total // amount), total * weights[0] // sum(weights)))
    least = 1 if total - largest >= amount - 1 else 0
    given, rest = [largest] + [least] * (amount - 1), total - largest - least * (amount - 1)
    while rest > 0:
        candidates = [i for i in range(1, amount) if given[i] < largest] or [i for i in range(1, amount) if given[i] < reach]
        whole, left = sum([weights[i] for i in candidates]), rest
        for i in candidates:
            more = min(reach - given[i], max(1, left * weights[i] // whole), rest)
            given[i] = given[i] + more
            rest = rest - more
    return np.array(given)


def centred(key, extent, spread, reach, cuts=(), kind=jnp.bfloat16):
    result = spread * jax.random.normal(key, extent, jnp.float32)
    if cuts:
        result = result * steps_of(key, extent, cuts, -0.22, 0.18)
    return jnp.clip(result, -reach, reach).astype(kind)


def setup_inputs(seed: int = 0) -> dict:
    keys = jax.random.split(jax.random.key(seed), 10)
    panel_nodes = draw_panel_nodes(jax.random.fold_in(keys[9], 71), 0)
    density = centred(keys[1], (PANELS * NODES,), 1.0, 6.0, ((0, 128),), jnp.float32)
    crevice_routes_keys = jax.random.split(jax.random.fold_in(keys[2], 1), PANELS // P_DEV)
    crevice_routes_turns = jax.random.permutation(jax.random.fold_in(keys[2], 3), PANELS // P_DEV)
    crevice_routes = jax.vmap(lambda own, number: assign_block(jax.random.fold_in(keys[2], 2), own, number, P_DEV, DEVICES, TOP, MOST, 2))(crevice_routes_keys, crevice_routes_turns).reshape((PANELS, TOP))
    crevice_centre = place_ends(jax.random.randint(keys[3], (PANELS, TOP), 0, C_DEV), jax.random.fold_in(keys[3], 1), 0, C_DEV - 1).astype(jnp.int32)
    centres = draw_centres(jax.random.fold_in(keys[9], 71), 0)
    targets = draw_targets(jax.random.fold_in(keys[9], 71), 0)
    centre_home_keys = jax.random.split(jax.random.fold_in(keys[6], 1), CENTRES // C_DEV)
    centre_home_turns = jax.random.permutation(jax.random.fold_in(keys[6], 3), CENTRES // C_DEV)
    centre_home = jax.vmap(lambda own, number: assign_block(jax.random.fold_in(keys[6], 2), own, number, C_DEV, DEVICES, 1, MOST_BACK, 1))(centre_home_keys, centre_home_turns).reshape((CENTRES, 1))
    upsample = draw_upsample(jax.random.fold_in(keys[9], 71), 0)
    fine_weights = jnp.clip(jnp.exp(jax.random.uniform(keys[8], (FINE,), jnp.float32, math.log(0.005), math.log(0.05))), 0.005, 0.05)
    return {"panel_nodes": panel_nodes, "density": density, "crevice_routes": crevice_routes, "crevice_centre": crevice_centre, "centres": centres, "targets": targets, "centre_home": centre_home, "upsample": upsample, "fine_weights": fine_weights}


def route_rank(destination, count):
    onehot = (destination[:, None] == jnp.arange(count, dtype=jnp.int32)[None, :]).astype(jnp.int32)
    before = jnp.cumsum(onehot, axis=0) - onehot
    return lax.optimization_barrier(jnp.sum(before * onehot, axis=1)).astype(jnp.int32)

def refine(coarse_all, upsample, fine_weights):
    upper = jnp.einsum('sck,nk->scn', coarse_all, upsample, precision=lax.Precision.HIGHEST)
    strength = upper[:, 3, :] * fine_weights[None, :]
    return jnp.concatenate([upper[:, :3, :], strength[:, None, :]], axis=1)

def expansion_terms(sources, centre_pos, target_pos):
    src_vec = sources[:, :3, :] - centre_pos[:, :, None]
    tgt_vec = target_pos - centre_pos[:, :, None]
    src_dist = jnp.sqrt(lax.optimization_barrier(jnp.sum(src_vec * src_vec, axis=1)))
    tgt_dist = jnp.sqrt(lax.optimization_barrier(jnp.sum(tgt_vec * tgt_vec, axis=1)))
    inner = lax.optimization_barrier(jnp.sum(src_vec[:, :, :, None] * tgt_vec[:, :, None, :], axis=1))
    cosine = inner / (src_dist[:, :, None] * tgt_dist[:, None, :])
    ratio = tgt_dist[:, None, :] / src_dist[:, :, None]
    p_prev = jnp.ones_like(cosine)
    p_now = cosine
    power = ratio
    total = 1.0 + ratio * cosine
    for level in range(1, ORDER):
        p_next = ((2 * level + 1) * cosine * p_now - level * p_prev) / (level + 1)
        power = power * ratio
        total = total + power * p_next
        p_prev, p_now = (p_now, p_next)
    kernel = total / src_dist[:, :, None]
    return lax.optimization_barrier(jnp.sum(sources[:, 3, :, None] * kernel, axis=1))

def reference(panel_nodes, density, crevice_routes, crevice_centre, centres, targets, centre_home, upsample, fine_weights):
    coarse_all = jnp.concatenate([panel_nodes.reshape(3, PANELS, NODES).transpose(1, 0, 2), density.reshape(PANELS, 1, NODES)], axis=1)
    target_all = targets.reshape(3, CENTRES, NODES)
    pairs = PANELS * TOP
    block = math.gcd(pairs, 4096)
    panel_of = (jnp.arange(pairs, dtype=jnp.int32) // TOP).astype(jnp.int32)
    centre_of = (crevice_routes.reshape(-1) * C_DEV + crevice_centre.reshape(-1)).astype(jnp.int32)

    def one_block(indices):
        panel_ids, centre_ids = indices
        sources = refine(coarse_all[panel_ids], upsample, fine_weights)
        centre_pos = centres[:, centre_ids].T
        target_pos = target_all[:, centre_ids, :].transpose(1, 0, 2)
        return expansion_terms(sources, centre_pos, target_pos)
    terms = lax.map(one_block, (panel_of.reshape(-1, block), centre_of.reshape(-1, block)))
    potential = jax.ops.segment_sum(terms.reshape(pairs, NODES), centre_of, num_segments=CENTRES)
    home = centre_home.reshape(DEVICES, C_DEV)
    rank = jax.vmap(lambda row: route_rank(row, DEVICES))(home)
    owner = jnp.arange(DEVICES, dtype=jnp.int32)[:, None]
    flat_index = ((home * DEVICES + owner) * MOST_BACK + rank).astype(jnp.int32)
    returned = jnp.zeros((DEVICES * DEVICES * MOST_BACK, NODES), jnp.float32).at[flat_index.reshape(-1)].set(potential)
    return returned.reshape(-1)
```

```python
import functools
import math

import jax
import jax.numpy as jnp
from jax import lax
from jax.experimental import pallas as pl
from jax.experimental.pallas import tpu as pltpu
from jax.sharding import PartitionSpec as P

MESH = pl.DeviceIdType.MESH
F32, BF16 = jnp.float32, jnp.bfloat16
ORDER = 8
NODES = 16
FINE = 64
NN = (((1,), (0,)), ((), ()))
NT = (((1,), (1,)), ((), ()))
TERMS = [(m, l) for m in range(ORDER + 1) for l in range(m, ORDER + 1)]
ROWS = 88


def rows_of():
    at, place = {}, 0
    for m in range(ORDER + 1):
        for l in range(m, ORDER + 1):
            for part in range(1 if m == 0 else 2):
                at[(m, l, part)] = place
                place += 1
    return at


PLACE = rows_of()


def weight(l, m):
    lead = math.factorial(2 * l) / (2**l * math.factorial(l) * math.factorial(l - m))
    return (1 if m == 0 else 2) * math.factorial(l - m) / math.factorial(l + m) * lead * lead


def harmonics(x, y, z, sq, start, emit):
    re, im = start, None
    for m in range(ORDER + 1):
        if m == 1:
            re, im = x * start, y * start
        elif m > 1:
            re, im = x * re - y * im, x * im + y * re
        old_re = old_im = None
        now_re, now_im = re, im
        for l in range(m, ORDER + 1):
            emit(m, l, 0, now_re)
            if m:
                emit(m, l, 1, now_im)
            if l == ORDER:
                break
            next_re = z * now_re
            next_im = z * now_im if m else None
            if l > m:
                damp = sq * ((l * l - m * m) / (4.0 * l * l - 1.0))
                next_re = next_re - damp * old_re
                if m:
                    next_im = next_im - damp * old_im
            old_re, old_im, now_re, now_im = now_re, now_im, next_re, next_im


def split3(value):
    hi = value.astype(BF16)
    rest = value - hi.astype(F32)
    mid = rest.astype(BF16)
    return hi, mid, (rest - mid.astype(F32)).astype(BF16)


def dot(a, b, dims=NN):
    return lax.dot_general(a, b, dims, preferred_element_type=F32)


def iota(shape, axis):
    return lax.broadcasted_iota(jnp.int32, shape, axis)


def kernel(
    grp_size,
    dev_size,
    pay_ref,
    routes_ref,
    ids_ref,
    home_ref,
    centres_ref,
    targets_ref,
    up_ref,
    fw_ref,
    out_ref,
    rank_scr,
    value_scr,
    out_box,
    in_box,
    back_box,
    table,
    pick_back,
    moments,
    local,
    send_sem,
    recv_sem,
    back_send_sem,
    back_recv_sem,
):
    n = grp_size * dev_size
    panels = pay_ref.shape[0]
    count = centres_ref.shape[1]
    groups = n // 8
    me = lax.axis_index("grp") * dev_size + lax.axis_index("dev")

    def device(p):
        return (p // dev_size, p % dev_size)

    barrier = pltpu.get_barrier_semaphore()

    def greet(i, carry):
        pl.semaphore_signal(barrier, inc=1, device_id=device((me + i) % n), device_id_type=MESH)
        return carry

    lax.fori_loop(1, n, greet, 0)

    owner = iota((n, panels), 0)
    first, second = owner == routes_ref[0:1, :], owner == routes_ref[1:2, :]
    named = first | second
    earlier = (iota((panels, panels), 0) < iota((panels, panels), 1)).astype(F32).astype(BF16)
    rank = dot(named.astype(F32).astype(BF16), earlier)
    rank_scr[...] = jnp.where(named, rank, -1.0)
    ids = ids_ref[...].astype(F32) - 256.0
    value_scr[...] = jnp.where(first, ids[0:1, :], jnp.where(second, ids[1:2, :], 0.0))
    pay = pay_ref[...]
    parts = jnp.concatenate(split3(jnp.concatenate([pay, pay], axis=1)), axis=1)
    ones = jnp.ones((panels, 128), BF16)
    block = 16
    left = iota((block * 8, 128), 1) < 64
    own_row = iota((block * 8, 128), 1) % 8 == iota((block * 8, 128), 0) % 8
    row8 = iota((8, panels), 0).astype(F32)

    def build(step, carry):
        base = step * block
        low, high, low_id, high_id = [], [], [], []
        for d in range(block):
            slot = jnp.broadcast_to(rank_scr[pl.ds(base + d, 1), :], (8, panels))
            value = jnp.broadcast_to(value_scr[pl.ds(base + d, 1), :], (8, panels))
            is_low, is_high = slot == row8, slot == row8 + 8.0
            low.append(jnp.where(is_low, 1.0, 0.0))
            high.append(jnp.where(is_high, 1.0, 0.0))
            low_id.append(jnp.where(is_low, value, 0.0))
            high_id.append(jnp.where(is_high, value, 0.0))

        def gather(pieces, what):
            return dot(jnp.concatenate(pieces, axis=0).astype(BF16), what)

        a, b = gather(low, parts), gather(high, parts)
        a = a[:, 0:128] + a[:, 128:256] + a[:, 256:384]
        b = b[:, 0:128] + b[:, 128:256] + b[:, 256:384]
        out_box[pl.ds(base, block), 0:8, :] = jnp.where(left, a, b).reshape(block, 8, 128)
        named_id = jnp.where(left, gather(low_id, ones), gather(high_id, ones)) + 256.0
        named_id = jnp.where(own_row, named_id, 0.0).reshape(block, 8, 128)
        out_box[pl.ds(base, block), 8, :] = jnp.sum(named_id, axis=1)
        return carry

    lax.fori_loop(0, n // block, build, 0)

    pl.semaphore_wait(barrier, n - 1)

    def send(i, carry):
        p = (me + i) % n
        pltpu.make_async_remote_copy(
            src_ref=out_box.at[p],
            dst_ref=in_box.at[me],
            send_sem=send_sem,
            recv_sem=recv_sem.at[me // 8],
            device_id=device(p),
            device_id_type=MESH,
        ).start()
        return carry

    lax.fori_loop(1, n, send, 0)
    pltpu.make_async_copy(out_box.at[me], in_box.at[me], recv_sem.at[me // 8]).start()

    home = iota((n, count), 0) == home_ref[...]
    home_rank = jnp.where(home, dot(home.astype(F32).astype(BF16), earlier), -1.0)
    for r in range(8):
        pick_back[n * r : n * (r + 1), :] = jnp.where(home_rank == float(r), 1.0, 0.0).astype(BF16)
    centres = centres_ref[...]
    tx = targets_ref[0:16, :] - centres[0:1, :]
    ty = targets_ref[16:32, :] - centres[1:2, :]
    tz = targets_ref[32:48, :] - centres[2:3, :]

    def keep(m, l, part, value):
        table[PLACE[(m, l, part)]] = value * weight(l, m)

    harmonics(tx, ty, tz, tx * tx + ty * ty + tz * tz, jnp.ones_like(tx), keep)
    padded = jnp.concatenate([centres, jnp.zeros((5, count), F32)], axis=0)
    centre_parts = jnp.concatenate(
        [part.astype(F32) for part in split3(padded)] + [jnp.zeros((8, count), F32)], axis=0
    ).astype(BF16)
    lanes = jnp.concatenate([up_ref[...]] * 8, axis=0)
    is_density = (iota(lanes.shape, 0) // NODES) % 4 == 3
    lanes = jnp.where(is_density, lanes * fw_ref[...], lanes)
    lanes = jnp.concatenate([lanes, lanes], axis=1).T[0:FINE, :]
    which = (iota(lanes.shape, 1) // NODES) % 4
    up = jnp.concatenate([jnp.where(which == c, lanes, 0.0) for c in range(4)], axis=0)
    up_hi, up_mid, up_lo = split3(up)
    up_a = jnp.concatenate([up_hi, up_hi], axis=1)
    up_b = jnp.concatenate([up_mid, up_mid], axis=1)
    up_c = jnp.concatenate([up_hi, up_lo], axis=1)
    local[...] = jnp.zeros_like(local)
    moments[...] = jnp.zeros_like(moments)
    lane64 = iota((64, 128), 1) < 64
    source_row = (iota((8, 128), 1) // 8) % 8 == iota((8, 128), 0)
    index = iota((count, 128), 0).astype(F32)

    def work(step, carry):
        q = (me // 8 + groups - step) % groups
        pltpu.make_async_copy(
            out_box.at[pl.ds(0, 8)], in_box.at[pl.ds(q * 8, 8)], recv_sem.at[q]
        ).wait()
        rows = in_box[pl.ds(q * 8, 8), 0:8, :].reshape(64, 128)
        rows = jnp.concatenate([jnp.where(lane64, rows, 0.0), jnp.where(lane64, 0.0, rows)], axis=0)
        hi, mid, lo = split3(rows)
        fine = dot(up_a, jnp.concatenate([hi, mid], axis=1), NT)
        fine = fine + dot(up_b, jnp.concatenate([hi, mid], axis=1), NT)
        fine = fine + dot(up_c, jnp.concatenate([lo, hi], axis=1), NT)
        named = in_box[pl.ds(q * 8, 8), 8, :]
        named = jnp.sum(jnp.where(source_row, named, 0.0), axis=0, keepdims=True)
        pick = jnp.where(index == named, 1.0, 0.0).astype(BF16)
        centre = dot(centre_parts, pick)
        centre = centre[0:8, :] + centre[8:16, :] + centre[16:24, :]
        part_rows = 32
        for piece in range(FINE // part_rows):
            at = piece * part_rows
            x = fine[at : at + part_rows, :] - centre[0:1, :]
            y = fine[FINE + at : FINE + at + part_rows, :] - centre[1:2, :]
            z = fine[2 * FINE + at : 2 * FINE + at + part_rows, :] - centre[2:3, :]
            strength = fine[3 * FINE + at : 3 * FINE + at + part_rows, :]
            dist = jnp.maximum(x * x + y * y + z * z, 0.01)
            inverse = 1.0 / dist
            start = strength * jnp.sqrt(inverse)

            def add(m, l, part, value):
                total = value[0:8, :]
                for k in range(1, part_rows // 8):
                    total = total + value[8 * k : 8 * k + 8, :]
                place = PLACE[(m, l, part)] * 8
                if piece:
                    total = total + moments[place : place + 8, :]
                moments[place : place + 8, :] = total

            harmonics(x * inverse, y * inverse, z * inverse, inverse, start, add)
        total = moments[pl.ds(0, ROWS, stride=8), :]
        for k in range(1, 8):
            total = total + moments[pl.ds(k, ROWS, stride=8), :]
        stacked = jnp.concatenate([part.astype(F32) for part in split3(total)], axis=0).astype(BF16)
        local[...] += dot(stacked, pick, NT)
        return carry

    lax.fori_loop(0, groups, work, 0)

    potential = jnp.zeros((NODES, count), F32)
    for place in range(len(PLACE)):
        coefficient = (
            local[place : place + 1, :]
            + local[ROWS + place : ROWS + place + 1, :]
            + local[2 * ROWS + place : 2 * ROWS + place + 1, :]
        )
        potential = potential + table[place] * coefficient
    back = jnp.concatenate([potential] * 8, axis=0)
    back = jnp.concatenate([part.astype(F32) for part in split3(back)], axis=0).astype(BF16)
    lane_slot = iota((n, 128), 1) // NODES
    answer = jnp.zeros((n, 128), F32)
    for r in range(8):
        found = dot(pick_back[n * r : n * (r + 1), :], back, NT)
        found = found[:, 0:128] + found[:, 128:256] + found[:, 256:384]
        answer = jnp.where(lane_slot == r, found, answer)
    back_box[...] = answer.reshape(n, 1, 128)

    def send_back(i, carry):
        p = (me + i) % n
        pltpu.make_async_remote_copy(
            src_ref=back_box.at[p],
            dst_ref=out_ref.at[me],
            send_sem=back_send_sem,
            recv_sem=back_recv_sem,
            device_id=device(p),
            device_id_type=MESH,
        ).start()
        return carry

    lax.fori_loop(1, n, send_back, 0)
    pltpu.make_async_copy(back_box.at[me], out_ref.at[me], back_recv_sem).start()
    pltpu.make_async_copy(
        out_box.at[pl.ds(0, n - 1)], in_box.at[pl.ds(0, n - 1)], send_sem
    ).wait()
    pltpu.make_async_copy(
        back_box.at[pl.ds(0, n - 1)], out_ref.at[pl.ds(0, n - 1)], back_send_sem
    ).wait()
    pltpu.make_async_copy(back_box, out_ref, back_recv_sem).wait()


def per_device(
    grp_size,
    dev_size,
    panel_nodes,
    density,
    crevice_routes,
    crevice_centre,
    centres,
    targets,
    centre_home,
    upsample,
    fine_weights,
):
    n = grp_size * dev_size
    panels = crevice_routes.shape[0]
    count = centres.shape[1]
    pay = jnp.concatenate(
        [
            panel_nodes.reshape(3, panels, NODES).transpose(1, 0, 2).reshape(panels, 3 * NODES),
            density.reshape(panels, NODES),
        ],
        axis=1,
    )
    tall = targets.reshape(3, count, NODES).transpose(0, 2, 1).reshape(3 * NODES, count)
    vmem = pl.BlockSpec(memory_space=pltpu.VMEM)
    returned = pl.pallas_call(
        functools.partial(kernel, grp_size, dev_size),
        out_shape=jax.ShapeDtypeStruct((n, 1, 128), F32),
        in_specs=[vmem] * 8,
        out_specs=vmem,
        scratch_shapes=[
            pltpu.VMEM((n, panels), F32),
            pltpu.VMEM((n, panels), F32),
            pltpu.VMEM((n, 9, 128), F32),
            pltpu.VMEM((n, 9, 128), F32),
            pltpu.VMEM((n, 1, 128), F32),
            pltpu.VMEM((len(PLACE), NODES, count), F32),
            pltpu.VMEM((8 * n, count), BF16),
            pltpu.VMEM((ROWS * 8, 128), F32),
            pltpu.VMEM((3 * ROWS, count), F32),
            pltpu.SemaphoreType.DMA,
            pltpu.SemaphoreType.DMA((n // 8,)),
            pltpu.SemaphoreType.DMA,
            pltpu.SemaphoreType.DMA,
        ],
        compiler_params=pltpu.CompilerParams(
            collective_id=0, has_side_effects=True, vmem_limit_bytes=48 << 20
        ),
    )(
        pay,
        crevice_routes.T,
        crevice_centre.T,
        centre_home.reshape(1, count),
        centres,
        tall,
        upsample.T,
        fine_weights.reshape(1, FINE),
    )
    return returned.reshape(-1)


def solution(mesh):
    split = P(None, ("grp", "dev"))
    rows = P(("grp", "dev"), None)
    placed = (split, P(("grp", "dev")), rows, rows, split, split, rows, P(), P())
    return jax.shard_map(
        functools.partial(per_device, mesh.shape["grp"], mesh.shape["dev"]),
        mesh=mesh,
        in_specs=placed,
        out_specs=P(("grp", "dev")),
        check_vma=False,
    )
```

```python
import functools
import math

import jax
import jax.numpy as jnp
from jax import lax
from jax.experimental import pallas as pl
from jax.experimental.pallas import tpu as pltpu
from jax.sharding import PartitionSpec as P

MESH = pl.DeviceIdType.MESH
F32, BF16 = jnp.float32, jnp.bfloat16
ORDER = 8
NODES = 16
FINE = 64
NN = (((1,), (0,)), ((), ()))
NT = (((1,), (1,)), ((), ()))
TERMS = [(m, l) for m in range(ORDER + 1) for l in range(m, ORDER + 1)]
ROWS = 88


def rows_of():
    at, place = {}, 0
    for m in range(ORDER + 1):
        for l in range(m, ORDER + 1):
            for part in range(1 if m == 0 else 2):
                at[(m, l, part)] = place
                place += 1
    return at


PLACE = rows_of()


def weight(l, m):
    lead = math.factorial(2 * l) / (2**l * math.factorial(l) * math.factorial(l - m))
    return (1 if m == 0 else 2) * math.factorial(l - m) / math.factorial(l + m) * lead * lead


def harmonics(x, y, z, sq, start, emit):
    re, im = start, None
    for m in range(ORDER + 1):
        if m == 1:
            re, im = x * start, y * start
        elif m > 1:
            re, im = x * re - y * im, x * im + y * re
        old_re = old_im = None
        now_re, now_im = re, im
        for l in range(m, ORDER + 1):
            emit(m, l, 0, now_re)
            if m:
                emit(m, l, 1, now_im)
            if l == ORDER:
                break
            next_re = z * now_re
            next_im = z * now_im if m else None
            if l > m:
                damp = sq * ((l * l - m * m) / (4.0 * l * l - 1.0))
                next_re = next_re - damp * old_re
                if m:
                    next_im = next_im - damp * old_im
            old_re, old_im, now_re, now_im = now_re, now_im, next_re, next_im


def split3(value):
    hi = value.astype(BF16)
    rest = value - hi.astype(F32)
    mid = rest.astype(BF16)
    return hi, mid, (rest - mid.astype(F32)).astype(BF16)


def dot(a, b, dims=NN):
    return lax.dot_general(a, b, dims, preferred_element_type=F32)


def iota(shape, axis):
    return lax.broadcasted_iota(jnp.int32, shape, axis)


def kernel(
    grp_size,
    dev_size,
    pay_ref,
    routes_ref,
    ids_ref,
    home_ref,
    centres_ref,
    targets_ref,
    up_ref,
    fw_ref,
    out_ref,
    rank_scr,
    value_scr,
    out_box,
    in_box,
    back_box,
    table,
    pick_back,
    up_ref2,
    points_a,
    points_b,
    pick_a,
    pick_b,
    moments_a,
    moments_b,
    local,
    send_sem,
    recv_sem,
    back_send_sem,
    back_recv_sem,
):
    n = grp_size * dev_size
    panels = pay_ref.shape[0]
    count = centres_ref.shape[1]
    groups = n // 8
    me = lax.axis_index("grp") * dev_size + lax.axis_index("dev")

    def device(p):
        return (p // dev_size, p % dev_size)

    barrier = pltpu.get_barrier_semaphore()

    def greet(i, carry):
        pl.semaphore_signal(barrier, inc=1, device_id=device((me + i) % n), device_id_type=MESH)
        return carry

    lax.fori_loop(1, n, greet, 0)

    owner = iota((n, panels), 0)
    first, second = owner == routes_ref[0:1, :], owner == routes_ref[1:2, :]
    named = first | second
    earlier = (iota((panels, panels), 0) < iota((panels, panels), 1)).astype(F32).astype(BF16)
    rank = dot(named.astype(F32).astype(BF16), earlier)
    rank_scr[...] = jnp.where(named, rank, -1.0)
    ids = ids_ref[...].astype(F32) - 256.0
    value_scr[...] = jnp.where(first, ids[0:1, :], jnp.where(second, ids[1:2, :], 0.0))
    pay = pay_ref[...]
    parts = jnp.concatenate(split3(jnp.concatenate([pay, pay], axis=1)), axis=1)
    ones = jnp.ones((panels, 128), BF16)
    block = 16
    left = iota((block * 8, 128), 1) < 64
    own_row = iota((block * 8, 128), 1) % 8 == iota((block * 8, 128), 0) % 8
    row8 = iota((8, panels), 0).astype(F32)

    def build(step, carry):
        base = step * block
        low, high, low_id, high_id = [], [], [], []
        for d in range(block):
            slot = jnp.broadcast_to(rank_scr[pl.ds(base + d, 1), :], (8, panels))
            value = jnp.broadcast_to(value_scr[pl.ds(base + d, 1), :], (8, panels))
            is_low, is_high = slot == row8, slot == row8 + 8.0
            low.append(jnp.where(is_low, 1.0, 0.0))
            high.append(jnp.where(is_high, 1.0, 0.0))
            low_id.append(jnp.where(is_low, value, 0.0))
            high_id.append(jnp.where(is_high, value, 0.0))

        def gather(pieces, what):
            return dot(jnp.concatenate(pieces, axis=0).astype(BF16), what)

        a, b = gather(low, parts), gather(high, parts)
        a = a[:, 0:128] + a[:, 128:256] + a[:, 256:384]
        b = b[:, 0:128] + b[:, 128:256] + b[:, 256:384]
        out_box[pl.ds(base, block), 0:8, :] = jnp.where(left, a, b).reshape(block, 8, 128)
        named_id = jnp.where(left, gather(low_id, ones), gather(high_id, ones)) + 256.0
        named_id = jnp.where(own_row, named_id, 0.0).reshape(block, 8, 128)
        out_box[pl.ds(base, block), 8, :] = jnp.sum(named_id, axis=1)
        return carry

    lax.fori_loop(0, n // block, build, 0)

    pl.semaphore_wait(barrier, n - 1)

    def send(i, carry):
        p = (me + i) % n
        pltpu.make_async_remote_copy(
            src_ref=out_box.at[p],
            dst_ref=in_box.at[me],
            send_sem=send_sem,
            recv_sem=recv_sem.at[me // 8],
            device_id=device(p),
            device_id_type=MESH,
        ).start()
        return carry

    lax.fori_loop(1, n, send, 0)
    pltpu.make_async_copy(out_box.at[me], in_box.at[me], recv_sem.at[me // 8]).start()

    home = iota((n, count), 0) == home_ref[...]
    home_rank = jnp.where(home, dot(home.astype(F32).astype(BF16), earlier), -1.0)
    for r in range(8):
        pick_back[n * r : n * (r + 1), :] = jnp.where(home_rank == float(r), 1.0, 0.0).astype(BF16)
    centres = centres_ref[...]
    tx = targets_ref[0:16, :] - centres[0:1, :]
    ty = targets_ref[16:32, :] - centres[1:2, :]
    tz = targets_ref[32:48, :] - centres[2:3, :]

    def keep(m, l, part, value):
        table[PLACE[(m, l, part)]] = value * weight(l, m)

    harmonics(tx, ty, tz, tx * tx + ty * ty + tz * tz, jnp.ones_like(tx), keep)
    padded = jnp.concatenate([centres, jnp.zeros((5, count), F32)], axis=0)
    centre_parts = jnp.concatenate(
        [part.astype(F32) for part in split3(padded)] + [jnp.zeros((8, count), F32)], axis=0
    ).astype(BF16)
    lanes = jnp.concatenate([up_ref[...]] * 8, axis=0)
    is_density = (iota(lanes.shape, 0) // NODES) % 4 == 3
    lanes = jnp.where(is_density, lanes * fw_ref[...], lanes)
    lanes = jnp.concatenate([lanes, lanes], axis=1).T[0:FINE, :]
    which = (iota(lanes.shape, 1) // NODES) % 4
    up = jnp.concatenate([jnp.where(which == c, lanes, 0.0) for c in range(4)], axis=0)
    up_hi, up_mid, _ = split3(up)
    up_ref2[...] = jnp.concatenate([up_hi, up_hi, up_mid, up_mid], axis=1)
    local[...] = jnp.zeros_like(local)
    moments_a[...] = jnp.zeros_like(moments_a)
    moments_b[...] = jnp.zeros_like(moments_b)
    pick_b[...] = jnp.zeros_like(pick_b)
    lane64 = iota((64, 128), 1) < 64
    source_row = (iota((8, 128), 1) // 8) % 8 == iota((8, 128), 0)
    index = iota((count, 128), 0).astype(F32)

    def prepare(step, points, pick):
        q = (me // 8 + groups - step) % groups
        pltpu.make_async_copy(
            out_box.at[pl.ds(0, 8)], in_box.at[pl.ds(q * 8, 8)], recv_sem.at[q]
        ).wait()
        rows = in_box[pl.ds(q * 8, 8), 0:8, :].reshape(64, 128)
        rows = jnp.concatenate([jnp.where(lane64, rows, 0.0), jnp.where(lane64, 0.0, rows)], axis=0)
        hi = rows.astype(BF16)
        mid = (rows - hi.astype(F32)).astype(BF16)
        both = jnp.concatenate([hi, mid, hi, mid], axis=1)
        fine = dot(up_ref2[...], both, NT)
        named = in_box[pl.ds(q * 8, 8), 8, :]
        named = jnp.sum(jnp.where(source_row, named, 0.0), axis=0, keepdims=True)
        picked = jnp.where(index == named, 1.0, 0.0).astype(BF16)
        centre = dot(centre_parts, picked)
        centre = centre[0:8, :] + centre[8:16, :] + centre[16:24, :]
        pick[:, 0:128] = picked
        pick[:, 128:256] = picked
        for c in range(3):
            points[c * FINE : (c + 1) * FINE, :] = fine[c * FINE : (c + 1) * FINE, :] - centre[c : c + 1, :]
        points[3 * FINE : 4 * FINE, :] = fine[3 * FINE : 4 * FINE, :]

    def expand(points, moments):
        part_rows = 32
        for piece in range(FINE // part_rows):
            at = piece * part_rows
            x = points[at : at + part_rows, :]
            y = points[FINE + at : FINE + at + part_rows, :]
            z = points[2 * FINE + at : 2 * FINE + at + part_rows, :]
            strength = points[3 * FINE + at : 3 * FINE + at + part_rows, :]
            dist = jnp.maximum(x * x + y * y + z * z, 0.01)
            inverse = 1.0 / dist
            start = strength * jnp.sqrt(inverse)

            def add(m, l, part, value):
                total = value[0:8, :]
                for k in range(1, part_rows // 8):
                    total = total + value[8 * k : 8 * k + 8, :]
                place = PLACE[(m, l, part)] * 8
                if piece:
                    total = total + moments[place : place + 8, :]
                moments[place : place + 8, :] = total

            harmonics(x * inverse, y * inverse, z * inverse, inverse, start, add)

    def gather(moments, pick):
        total = moments[pl.ds(0, ROWS, stride=8), :]
        for k in range(1, 8):
            total = total + moments[pl.ds(k, ROWS, stride=8), :]
        hi = total.astype(BF16).astype(F32)
        both = jnp.concatenate([hi, total - hi], axis=1).astype(BF16)
        local[...] += dot(both, pick[...], NT)

    prepare(0, points_a, pick_a)

    def pair(i, carry):
        gather(moments_b, pick_b)
        prepare(2 * i + 1, points_b, pick_b)
        expand(points_a, moments_a)
        gather(moments_a, pick_a)
        prepare(2 * i + 2, points_a, pick_a)
        expand(points_b, moments_b)
        return carry

    lax.fori_loop(0, groups // 2 - 1, pair, 0)
    gather(moments_b, pick_b)
    prepare(groups - 1, points_b, pick_b)
    expand(points_a, moments_a)
    gather(moments_a, pick_a)
    expand(points_b, moments_b)
    gather(moments_b, pick_b)

    potential = jnp.zeros((NODES, count), F32)
    for place in range(len(PLACE)):
        potential = potential + table[place] * local[place : place + 1, :]
    back = jnp.concatenate([potential] * 8, axis=0)
    back = jnp.concatenate([part.astype(F32) for part in split3(back)], axis=0).astype(BF16)
    lane_slot = iota((n, 128), 1) // NODES
    answer = jnp.zeros((n, 128), F32)
    for r in range(8):
        found = dot(pick_back[n * r : n * (r + 1), :], back, NT)
        found = found[:, 0:128] + found[:, 128:256] + found[:, 256:384]
        answer = jnp.where(lane_slot == r, found, answer)
    back_box[...] = answer.reshape(n, 1, 128)

    def send_back(i, carry):
        p = (me + i) % n
        pltpu.make_async_remote_copy(
            src_ref=back_box.at[p],
            dst_ref=out_ref.at[me],
            send_sem=back_send_sem,
            recv_sem=back_recv_sem,
            device_id=device(p),
            device_id_type=MESH,
        ).start()
        return carry

    lax.fori_loop(1, n, send_back, 0)
    pltpu.make_async_copy(back_box.at[me], out_ref.at[me], back_recv_sem).start()
    pltpu.make_async_copy(
        out_box.at[pl.ds(0, n - 1)], in_box.at[pl.ds(0, n - 1)], send_sem
    ).wait()
    pltpu.make_async_copy(
        back_box.at[pl.ds(0, n - 1)], out_ref.at[pl.ds(0, n - 1)], back_send_sem
    ).wait()
    pltpu.make_async_copy(back_box, out_ref, back_recv_sem).wait()


def per_device(
    grp_size,
    dev_size,
    panel_nodes,
    density,
    crevice_routes,
    crevice_centre,
    centres,
    targets,
    centre_home,
    upsample,
    fine_weights,
):
    n = grp_size * dev_size
    panels = crevice_routes.shape[0]
    count = centres.shape[1]
    pay = jnp.concatenate(
        [
            panel_nodes.reshape(3, panels, NODES).transpose(1, 0, 2).reshape(panels, 3 * NODES),
            density.reshape(panels, NODES),
        ],
        axis=1,
    )
    tall = targets.reshape(3, count, NODES).transpose(0, 2, 1).reshape(3 * NODES, count)
    vmem = pl.BlockSpec(memory_space=pltpu.VMEM)
    returned = pl.pallas_call(
        functools.partial(kernel, grp_size, dev_size),
        out_shape=jax.ShapeDtypeStruct((n, 1, 128), F32),
        in_specs=[vmem] * 8,
        out_specs=vmem,
        scratch_shapes=[
            pltpu.VMEM((n, panels), F32),
            pltpu.VMEM((n, panels), F32),
            pltpu.VMEM((n, 9, 128), F32),
            pltpu.VMEM((n, 9, 128), F32),
            pltpu.VMEM((n, 1, 128), F32),
            pltpu.VMEM((len(PLACE), NODES, count), F32),
            pltpu.VMEM((8 * n, count), BF16),
            pltpu.VMEM((4 * FINE, 512), BF16),
            pltpu.VMEM((4 * FINE, 128), F32),
            pltpu.VMEM((4 * FINE, 128), F32),
            pltpu.VMEM((count, 256), BF16),
            pltpu.VMEM((count, 256), BF16),
            pltpu.VMEM((ROWS * 8, 128), F32),
            pltpu.VMEM((ROWS * 8, 128), F32),
            pltpu.VMEM((ROWS, count), F32),
            pltpu.SemaphoreType.DMA,
            pltpu.SemaphoreType.DMA((n // 8,)),
            pltpu.SemaphoreType.DMA,
            pltpu.SemaphoreType.DMA,
        ],
        compiler_params=pltpu.CompilerParams(
            collective_id=0, has_side_effects=True, vmem_limit_bytes=48 << 20
        ),
    )(
        pay,
        crevice_routes.T,
        crevice_centre.T,
        centre_home.reshape(1, count),
        centres,
        tall,
        upsample.T,
        fine_weights.reshape(1, FINE),
    )
    return returned.reshape(-1)


def solution(mesh):
    split = P(None, ("grp", "dev"))
    rows = P(("grp", "dev"), None)
    placed = (split, P(("grp", "dev")), rows, rows, split, split, rows, P(), P())
    return jax.shard_map(
        functools.partial(per_device, mesh.shape["grp"], mesh.shape["dev"]),
        mesh=mesh,
        in_specs=placed,
        out_specs=P(("grp", "dev")),
        check_vma=False,
    )
```

```python
import functools
import math

import jax
import jax.numpy as jnp
from jax import lax
from jax.experimental import pallas as pl
from jax.experimental.pallas import tpu as pltpu
from jax.sharding import PartitionSpec as P

MESH = pl.DeviceIdType.MESH
F32, BF16 = jnp.float32, jnp.bfloat16
ORDER = 8
NODES = 16
FINE = 64
NN = (((1,), (0,)), ((), ()))
NT = (((1,), (1,)), ((), ()))
TERMS = [(m, l) for m in range(ORDER + 1) for l in range(m, ORDER + 1)]
ROWS = 88


def rows_of():
    at, place = {}, 0
    for m in range(ORDER + 1):
        for l in range(m, ORDER + 1):
            for part in range(1 if m == 0 else 2):
                at[(m, l, part)] = place
                place += 1
    return at


PLACE = rows_of()


def weight(l, m):
    lead = math.factorial(2 * l) / (2**l * math.factorial(l) * math.factorial(l - m))
    return (1 if m == 0 else 2) * math.factorial(l - m) / math.factorial(l + m) * lead * lead


def harmonics(x, y, z, sq, start, emit):
    re, im = start, None
    for m in range(ORDER + 1):
        if m == 1:
            re, im = x * start, y * start
        elif m > 1:
            re, im = x * re - y * im, x * im + y * re
        old_re = old_im = None
        now_re, now_im = re, im
        for l in range(m, ORDER + 1):
            emit(m, l, 0, now_re)
            if m:
                emit(m, l, 1, now_im)
            if l == ORDER:
                break
            next_re = z * now_re
            next_im = z * now_im if m else None
            if l > m:
                damp = sq * ((l * l - m * m) / (4.0 * l * l - 1.0))
                next_re = next_re - damp * old_re
                if m:
                    next_im = next_im - damp * old_im
            old_re, old_im, now_re, now_im = now_re, now_im, next_re, next_im


def split3(value):
    hi = value.astype(BF16)
    rest = value - hi.astype(F32)
    mid = rest.astype(BF16)
    return hi, mid, (rest - mid.astype(F32)).astype(BF16)


def dot(a, b, dims=NN):
    return lax.dot_general(a, b, dims, preferred_element_type=F32)


def iota(shape, axis):
    return lax.broadcasted_iota(jnp.int32, shape, axis)


def kernel(
    grp_size,
    dev_size,
    nodes_hbm,
    density_hbm,
    routes_hbm,
    ids_hbm,
    home_hbm,
    centres_hbm,
    targets_hbm,
    up_hbm,
    fw_hbm,
    out_ref,
    stage,
    pay_scr,
    pay_parts,
    rank_scr,
    rank_scr2,
    out_box,
    in_box,
    back_box,
    table,
    pick_back,
    up_ref2,
    points_a,
    points_b,
    pick_a,
    pick_b,
    moments_a,
    moments_b,
    local,
    send_sem,
    recv_sem,
    back_send_sem,
    back_recv_sem,
    nodes_ref,
    density_ref,
    routes_ref,
    ids_ref,
    home_ref,
    centres_ref,
    targets_ref,
    up_ref,
    fw_ref,
    load_sem,
):
    n = grp_size * dev_size
    loads = [
        pltpu.make_async_copy(source, copy, load_sem.at[i])
        for i, (source, copy) in enumerate(
            (
                (nodes_hbm, nodes_ref),
                (density_hbm, density_ref),
                (routes_hbm, routes_ref),
                (ids_hbm, ids_ref),
                (home_hbm, home_ref),
                (centres_hbm, centres_ref),
                (targets_hbm, targets_ref),
                (up_hbm, up_ref),
                (fw_hbm, fw_ref),
            )
        )
    ]
    for load in loads:
        load.start()
    panels = routes_ref.shape[1]
    count = centres_ref.shape[1]
    groups = n // 8
    me = lax.axis_index("grp") * dev_size + lax.axis_index("dev")

    def device(p):
        return (p // dev_size, p % dev_size)

    barrier = pltpu.get_barrier_semaphore()

    def greet(i, carry):
        pl.semaphore_signal(barrier, inc=1, device_id=device((me + i) % n), device_id_type=MESH)
        return carry

    lax.fori_loop(1, n, greet, 0, unroll=True)
    for load in loads[:4]:
        load.wait()

    lane = iota((64, 128), 1)
    for row in range(64):
        stage[row * 8 : row * 8 + 3, :] = nodes_ref[:, row * 128 : (row + 1) * 128]
    parts_of = [stage[pl.ds(c, 64, stride=8), :] for c in range(3)] + [density_ref[...]]
    turned = [[pltpu.roll(v, t * NODES, 1) if t else v for t in range(8)] for v in parts_of]
    for g in range(8):
        built = turned[0][(0 - g) % 8]
        for c in range(1, 8):
            built = jnp.where(lane // NODES == c, turned[c % 4][(c - g) % 8], built)
        pay_scr[pl.ds(g, 64, stride=8), :] = built
    owner = iota((n, panels), 0)
    first, second = owner == routes_ref[0:1, :], owner == routes_ref[1:2, :]
    named = first | second
    earlier = (iota((panels, panels), 0) < iota((panels, panels), 1)).astype(F32).astype(BF16)
    rank = dot(named.astype(F32).astype(BF16), earlier)
    rank_scr[...] = jnp.where(first, rank, -1.0)
    rank_scr2[...] = jnp.where(second, rank, -1.0)
    ids = ids_ref[...].astype(F32) - 256.0
    for block in range(panels // 128):
        at = block * 128
        square = jnp.concatenate(
            [jnp.broadcast_to(ids[r : r + 1, at : at + 128], (64, 128)) for r in range(2)], axis=0
        ).T
        hi, mid, lo = split3(pay_scr[at : at + 128, :])
        left = iota((128, 128), 1) < 64
        front = jnp.where(left, hi.astype(F32), mid.astype(F32)).astype(BF16)
        low = lo.astype(F32)
        pay_parts[at : at + 128, 0:128] = front
        pay_parts[panels + at : panels + at + 128, 0:128] = front
        pay_parts[at : at + 128, 128:256] = jnp.where(left, low, pltpu.roll(square, 64, 1)).astype(BF16)
        pay_parts[panels + at : panels + at + 128, 128:256] = jnp.where(left, low, square).astype(BF16)
    block = 32
    left = iota((block * 8, 128), 1) < 64
    own_row = iota((block * 8, 128), 1) % 8 == iota((block * 8, 128), 0) % 8
    row8 = iota((8, panels), 0).astype(F32)

    def build(step, carry):
        base = step * block
        low, high = [], []
        for d in range(block):
            slot = jnp.broadcast_to(rank_scr[pl.ds(base + d, 1), :], (8, panels))
            slot2 = jnp.broadcast_to(rank_scr2[pl.ds(base + d, 1), :], (8, panels))
            for rows, offset in ((low, 0.0), (high, 8.0)):
                rows.append(
                    jnp.concatenate(
                        [
                            jnp.where(slot == row8 + offset, 1.0, 0.0),
                            jnp.where(slot2 == row8 + offset, 1.0, 0.0),
                        ],
                        axis=1,
                    )
                )
        picked = dot(jnp.concatenate(low + high, axis=0).astype(BF16), pay_parts[...])
        front, rear = picked[:, 0:128], picked[:, 128:256]
        front = front + pltpu.roll(front, 64, 1)
        turned = pltpu.roll(rear, 64, 1)
        half = block * 8
        rows = jnp.where(left, front[:half] + rear[:half], front[half:] + turned[half:])
        out_box[pl.ds(base, block), 0:8, :] = rows.reshape(block, 8, 128)
        named_id = jnp.where(left, turned[:half], rear[half:]) + 256.0
        named_id = jnp.where(own_row, named_id, 0.0).reshape(block, 8, 128)
        out_box[pl.ds(base, block), 8, :] = jnp.sum(named_id, axis=1)
        return carry

    lax.fori_loop(0, n // block, build, 0)

    pl.semaphore_wait(barrier, n - 1)

    def send(i, carry):
        p = (me + i) % n
        pltpu.make_async_remote_copy(
            src_ref=out_box.at[p],
            dst_ref=in_box.at[me],
            send_sem=send_sem,
            recv_sem=recv_sem.at[me // 8],
            device_id=device(p),
            device_id_type=MESH,
        ).start()
        return carry

    lax.fori_loop(1, n, send, 0, unroll=True)
    pltpu.make_async_copy(out_box.at[me], in_box.at[me], recv_sem.at[me // 8]).start()

    for load in loads[4:]:
        load.wait()
    home = iota((n, count), 0) == home_ref[...]
    home_rank = jnp.where(home, dot(home.astype(F32).astype(BF16), earlier), -1.0)
    for r in range(8):
        pick_back[n * r : n * (r + 1), :] = jnp.where(home_rank == float(r), 1.0, 0.0).astype(BF16)
    centres = centres_ref[...]
    for row in range(64):
        stage[row * 8 : row * 8 + 3, :] = targets_ref[:, row * 128 : (row + 1) * 128]
    tall = [stage[pl.ds(c, 64, stride=8), :] for c in range(3)]
    blank = jnp.zeros((64, 128), F32)
    tall = [
        jnp.concatenate([tall[0], blank], axis=0).T,
        jnp.concatenate([blank, tall[1]], axis=0).T,
        jnp.concatenate([tall[2], blank], axis=0).T,
    ]
    tall = [part.astype(F32) for triple in zip(*[split3(v) for v in tall]) for part in triple]
    tall = jnp.concatenate(
        [
            jnp.concatenate([v[g * NODES : (g + 1) * NODES, :] for g in range(8)], axis=1)
            for v in tall
        ],
        axis=0,
    ).astype(BF16)
    spread = iota((8 * 128, count), 0)
    spread = (spread % 64) * 8 + spread // 128 == iota((8 * 128, count), 1)
    tall = dot(tall, jnp.where(spread, 1.0, 0.0).astype(BF16))
    tall = tall[0:48, :] + tall[48:96, :] + tall[96:144, :]
    tx = tall[0:16, :] - centres[0:1, :]
    ty = tall[16:32, :] - centres[1:2, :]
    tz = tall[32:48, :] - centres[2:3, :]

    def keep(m, l, part, value):
        table[PLACE[(m, l, part)]] = value * weight(l, m)

    harmonics(tx, ty, tz, tx * tx + ty * ty + tz * tz, jnp.ones_like(tx), keep)
    padded = jnp.concatenate([centres, jnp.zeros((5, count), F32)], axis=0)
    centre_parts = jnp.concatenate(
        [part.astype(F32) for part in split3(padded)] + [jnp.zeros((8, count), F32)], axis=0
    ).astype(BF16)
    lanes = jnp.concatenate([up_ref[...]] * 8, axis=0)
    is_density = (iota(lanes.shape, 0) // NODES) % 4 == 3
    lanes = jnp.where(is_density, lanes * fw_ref[...], lanes)
    lanes = jnp.concatenate([lanes, lanes], axis=1).T[0:FINE, :]
    which = (iota(lanes.shape, 1) // NODES) % 4
    up = jnp.concatenate([jnp.where(which == c, lanes, 0.0) for c in range(4)], axis=0)
    up_hi, up_mid, _ = split3(up)
    up_ref2[...] = jnp.concatenate([up_hi, up_hi, up_mid, up_mid], axis=1)
    local[...] = jnp.zeros_like(local)
    moments_a[...] = jnp.zeros_like(moments_a)
    moments_b[...] = jnp.zeros_like(moments_b)
    pick_b[...] = jnp.zeros_like(pick_b)
    lane64 = iota((64, 128), 1) < 64
    source_row = (iota((8, 128), 1) // 8) % 8 == iota((8, 128), 0)
    index = iota((count, 128), 0).astype(F32)

    def prepare(step, points, pick):
        q = (me // 8 + groups - step) % groups
        pltpu.make_async_copy(
            out_box.at[pl.ds(0, 8)], in_box.at[pl.ds(q * 8, 8)], recv_sem.at[q]
        ).wait()
        rows = in_box[pl.ds(q * 8, 8), 0:8, :].reshape(64, 128)
        rows = jnp.concatenate([jnp.where(lane64, rows, 0.0), jnp.where(lane64, 0.0, rows)], axis=0)
        hi = rows.astype(BF16)
        mid = (rows - hi.astype(F32)).astype(BF16)
        both = jnp.concatenate([hi, mid, hi, mid], axis=1)
        fine = dot(up_ref2[...], both, NT)
        named = in_box[pl.ds(q * 8, 8), 8, :]
        named = jnp.sum(jnp.where(source_row, named, 0.0), axis=0, keepdims=True)
        picked = jnp.where(index == named, 1.0, 0.0).astype(BF16)
        centre = dot(centre_parts, picked)
        centre = centre[0:8, :] + centre[8:16, :] + centre[16:24, :]
        pick[:, 0:128] = picked
        pick[:, 128:256] = picked
        for c in range(3):
            points[c * FINE : (c + 1) * FINE, :] = fine[c * FINE : (c + 1) * FINE, :] - centre[c : c + 1, :]
        points[3 * FINE : 4 * FINE, :] = fine[3 * FINE : 4 * FINE, :]

    def expand(points, moments):
        part_rows = 32
        for piece in range(FINE // part_rows):
            at = piece * part_rows
            x = points[at : at + part_rows, :]
            y = points[FINE + at : FINE + at + part_rows, :]
            z = points[2 * FINE + at : 2 * FINE + at + part_rows, :]
            strength = points[3 * FINE + at : 3 * FINE + at + part_rows, :]
            dist = jnp.maximum(x * x + y * y + z * z, 0.01)
            inverse = 1.0 / dist
            start = strength * jnp.sqrt(inverse)

            def add(m, l, part, value):
                total = value[0:8, :]
                for k in range(1, part_rows // 8):
                    total = total + value[8 * k : 8 * k + 8, :]
                place = PLACE[(m, l, part)] * 8
                if piece:
                    total = total + moments[place : place + 8, :]
                moments[place : place + 8, :] = total

            harmonics(x * inverse, y * inverse, z * inverse, inverse, start, add)

    def gather(moments, pick):
        total = moments[pl.ds(0, ROWS, stride=8), :]
        for k in range(1, 8):
            total = total + moments[pl.ds(k, ROWS, stride=8), :]
        hi = total.astype(BF16).astype(F32)
        both = jnp.concatenate([hi, total - hi], axis=1).astype(BF16)
        local[...] += dot(both, pick[...], NT)

    prepare(0, points_a, pick_a)

    def pair(i, carry):
        gather(moments_b, pick_b)
        prepare(2 * i + 1, points_b, pick_b)
        expand(points_a, moments_a)
        gather(moments_a, pick_a)
        prepare(2 * i + 2, points_a, pick_a)
        expand(points_b, moments_b)
        return carry

    lax.fori_loop(0, groups // 2 - 1, pair, 0)
    gather(moments_b, pick_b)
    prepare(groups - 1, points_b, pick_b)
    expand(points_a, moments_a)
    gather(moments_a, pick_a)
    expand(points_b, moments_b)
    gather(moments_b, pick_b)

    potential = jnp.zeros((NODES, count), F32)
    for place in range(len(PLACE)):
        potential = potential + table[place] * local[place : place + 1, :]
    back = jnp.concatenate([potential] * 8, axis=0)
    back = jnp.concatenate([part.astype(F32) for part in split3(back)], axis=0).astype(BF16)
    lane_slot = iota((n, 128), 1) // NODES
    answer = jnp.zeros((n, 128), F32)
    for r in range(8):
        found = dot(pick_back[n * r : n * (r + 1), :], back, NT)
        found = found[:, 0:128] + found[:, 128:256] + found[:, 256:384]
        answer = jnp.where(lane_slot == r, found, answer)
    back_box[...] = answer.reshape(n, 1, 128)

    def send_back(i, carry):
        p = (me + i) % n
        pltpu.make_async_remote_copy(
            src_ref=back_box.at[p],
            dst_ref=out_ref.at[me],
            send_sem=back_send_sem,
            recv_sem=back_recv_sem,
            device_id=device(p),
            device_id_type=MESH,
        ).start()
        return carry

    lax.fori_loop(1, n, send_back, 0, unroll=True)
    pltpu.make_async_copy(back_box.at[me], out_ref.at[me], back_recv_sem).start()
    pltpu.make_async_copy(
        out_box.at[pl.ds(0, n - 1)], in_box.at[pl.ds(0, n - 1)], send_sem
    ).wait()
    pltpu.make_async_copy(
        back_box.at[pl.ds(0, n - 1)], out_ref.at[pl.ds(0, n - 1)], back_send_sem
    ).wait()
    pltpu.make_async_copy(back_box, out_ref, back_recv_sem).wait()


def per_device(
    grp_size,
    dev_size,
    panel_nodes,
    density,
    crevice_routes,
    crevice_centre,
    centres,
    targets,
    centre_home,
    upsample,
    fine_weights,
):
    n = grp_size * dev_size
    panels = crevice_routes.shape[0]
    count = centres.shape[1]
    vmem = pl.BlockSpec(memory_space=pltpu.VMEM)
    returned = pl.pallas_call(
        functools.partial(kernel, grp_size, dev_size),
        out_shape=jax.ShapeDtypeStruct((n, 1, 128), F32),
        in_specs=[pl.BlockSpec(memory_space=pltpu.HBM)] * 9,
        out_specs=vmem,
        scratch_shapes=[
            pltpu.VMEM((512, 128), F32),
            pltpu.VMEM((panels, 128), F32),
            pltpu.VMEM((2 * panels, 256), BF16),
            pltpu.VMEM((n, panels), F32),
            pltpu.VMEM((n, panels), F32),
            pltpu.VMEM((n, 9, 128), F32),
            pltpu.VMEM((n, 9, 128), F32),
            pltpu.VMEM((n, 1, 128), F32),
            pltpu.VMEM((len(PLACE), NODES, count), F32),
            pltpu.VMEM((8 * n, count), BF16),
            pltpu.VMEM((4 * FINE, 512), BF16),
            pltpu.VMEM((4 * FINE, 128), F32),
            pltpu.VMEM((4 * FINE, 128), F32),
            pltpu.VMEM((count, 256), BF16),
            pltpu.VMEM((count, 256), BF16),
            pltpu.VMEM((ROWS * 8, 128), F32),
            pltpu.VMEM((ROWS * 8, 128), F32),
            pltpu.VMEM((ROWS, count), F32),
            pltpu.SemaphoreType.DMA,
            pltpu.SemaphoreType.DMA((n // 8,)),
            pltpu.SemaphoreType.DMA,
            pltpu.SemaphoreType.DMA,
            pltpu.VMEM((3, panels * NODES), F32),
            pltpu.VMEM((panels * NODES // 128, 128), F32),
            pltpu.VMEM((2, panels), jnp.int32),
            pltpu.VMEM((2, panels), jnp.int32),
            pltpu.VMEM((1, count), jnp.int32),
            pltpu.VMEM((3, count), F32),
            pltpu.VMEM((3, count * NODES), F32),
            pltpu.VMEM((NODES, FINE), F32),
            pltpu.VMEM((1, FINE), F32),
            pltpu.SemaphoreType.DMA((9,)),
        ],
        compiler_params=pltpu.CompilerParams(
            collective_id=0, has_side_effects=True, vmem_limit_bytes=58 << 20
        ),
    )(
        panel_nodes,
        density.reshape(panels * NODES // 128, 128),
        crevice_routes.T,
        crevice_centre.T,
        centre_home.reshape(1, count),
        centres,
        targets,
        upsample.T,
        fine_weights.reshape(1, FINE),
    )
    return returned.reshape(-1)


def solution(mesh):
    split = P(None, ("grp", "dev"))
    rows = P(("grp", "dev"), None)
    placed = (split, P(("grp", "dev")), rows, rows, split, split, rows, P(), P())
    return jax.shard_map(
        functools.partial(per_device, mesh.shape["grp"], mesh.shape["dev"]),
        mesh=mesh,
        in_specs=placed,
        out_specs=P(("grp", "dev")),
        check_vma=False,
    )
```

```python
import functools
import math

import jax
import jax.numpy as jnp
from jax import lax
from jax.experimental import pallas as pl
from jax.experimental.pallas import tpu as pltpu
from jax.sharding import PartitionSpec as P

MESH = pl.DeviceIdType.MESH
F32, BF16 = jnp.float32, jnp.bfloat16
ORDER = 8
NODES = 16
FINE = 64
NN = (((1,), (0,)), ((), ()))
NT = (((1,), (1,)), ((), ()))
TERMS = [(m, l) for m in range(ORDER + 1) for l in range(m, ORDER + 1)]
ROWS = 88


def rows_of():
    at, place = {}, 0
    for m in range(ORDER + 1):
        for l in range(m, ORDER + 1):
            for part in range(1 if m == 0 else 2):
                at[(m, l, part)] = place
                place += 1
    return at


PLACE = rows_of()


def weight(l, m):
    lead = math.factorial(2 * l) / (2**l * math.factorial(l) * math.factorial(l - m))
    return (1 if m == 0 else 2) * math.factorial(l - m) / math.factorial(l + m) * lead * lead


def harmonics(x, y, z, sq, start, emit):
    re, im = start, None
    for m in range(ORDER + 1):
        if m == 1:
            re, im = x * start, y * start
        elif m > 1:
            re, im = x * re - y * im, x * im + y * re
        old_re = old_im = None
        now_re, now_im = re, im
        for l in range(m, ORDER + 1):
            emit(m, l, 0, now_re)
            if m:
                emit(m, l, 1, now_im)
            if l == ORDER:
                break
            next_re = z * now_re
            next_im = z * now_im if m else None
            if l > m:
                damp = sq * ((l * l - m * m) / (4.0 * l * l - 1.0))
                next_re = next_re - damp * old_re
                if m:
                    next_im = next_im - damp * old_im
            old_re, old_im, now_re, now_im = now_re, now_im, next_re, next_im


def split3(value):
    hi = value.astype(BF16)
    rest = value - hi.astype(F32)
    mid = rest.astype(BF16)
    return hi, mid, (rest - mid.astype(F32)).astype(BF16)


def dot(a, b, dims=NN):
    return lax.dot_general(a, b, dims, preferred_element_type=F32)


def iota(shape, axis):
    return lax.broadcasted_iota(jnp.int32, shape, axis)


def kernel(
    grp_size,
    dev_size,
    nodes_hbm,
    density_hbm,
    routes_hbm,
    ids_hbm,
    home_hbm,
    centres_hbm,
    targets_hbm,
    up_hbm,
    fw_hbm,
    out_ref,
    stage,
    pay_scr,
    pay_parts,
    rank_scr,
    rank_scr2,
    out_box,
    in_box,
    back_box,
    table,
    pick_back,
    up_ref2,
    points_a,
    points_b,
    pick_a,
    pick_b,
    moments_a,
    moments_b,
    local,
    send_sem,
    recv_sem,
    back_send_sem,
    back_recv_sem,
    nodes_ref,
    density_ref,
    routes_ref,
    ids_ref,
    home_ref,
    centres_ref,
    targets_ref,
    up_ref,
    fw_ref,
    load_sem,
):
    n = grp_size * dev_size
    loads = [
        pltpu.make_async_copy(source, copy, load_sem.at[i])
        for i, (source, copy) in enumerate(
            (
                (nodes_hbm, nodes_ref),
                (density_hbm, density_ref),
                (routes_hbm, routes_ref),
                (ids_hbm, ids_ref),
                (home_hbm, home_ref),
                (centres_hbm, centres_ref),
                (targets_hbm, targets_ref),
                (up_hbm, up_ref),
                (fw_hbm, fw_ref),
            )
        )
    ]
    for load in loads:
        load.start()
    panels = routes_ref.shape[1]
    count = centres_ref.shape[1]
    groups = n // 8
    me = lax.axis_index("grp") * dev_size + lax.axis_index("dev")

    def device(p):
        return (p // dev_size, p % dev_size)

    barrier = pltpu.get_barrier_semaphore()

    def greet(i, carry):
        pl.semaphore_signal(barrier, inc=1, device_id=device((me + i) % n), device_id_type=MESH)
        return carry

    lax.fori_loop(1, n, greet, 0, unroll=True)
    for load in loads[:4]:
        load.wait()

    lane = iota((64, 128), 1)
    for row in range(64):
        stage[row * 8 : row * 8 + 3, :] = nodes_ref[:, row * 128 : (row + 1) * 128]
    parts_of = [stage[pl.ds(c, 64, stride=8), :] for c in range(3)] + [density_ref[...]]
    turned = [[pltpu.roll(v, t * NODES, 1) if t else v for t in range(8)] for v in parts_of]
    for g in range(8):
        built = turned[0][(0 - g) % 8]
        for c in range(1, 8):
            built = jnp.where(lane // NODES == c, turned[c % 4][(c - g) % 8], built)
        pay_scr[pl.ds(g, 64, stride=8), :] = built
    owner = iota((n, panels), 0)
    first, second = owner == routes_ref[0:1, :], owner == routes_ref[1:2, :]
    named = first | second
    earlier = (iota((panels, panels), 0) < iota((panels, panels), 1)).astype(F32).astype(BF16)
    rank = dot(named.astype(F32).astype(BF16), earlier)
    rank_scr[...] = jnp.where(first, rank, -1.0)
    rank_scr2[...] = jnp.where(second, rank, -1.0)
    ids = ids_ref[...].astype(F32) - 256.0
    for block in range(panels // 128):
        at = block * 128
        square = jnp.concatenate(
            [jnp.broadcast_to(ids[r : r + 1, at : at + 128], (64, 128)) for r in range(2)], axis=0
        ).T
        hi, mid, lo = split3(pay_scr[at : at + 128, :])
        left = iota((128, 128), 1) < 64
        front = jnp.where(left, hi.astype(F32), mid.astype(F32)).astype(BF16)
        low = lo.astype(F32)
        pay_parts[at : at + 128, 0:128] = front
        pay_parts[panels + at : panels + at + 128, 0:128] = front
        pay_parts[at : at + 128, 128:256] = jnp.where(left, low, pltpu.roll(square, 64, 1)).astype(BF16)
        pay_parts[panels + at : panels + at + 128, 128:256] = jnp.where(left, low, square).astype(BF16)
    block = 32
    left = iota((block * 8, 128), 1) < 64
    own_row = iota((block * 8, 128), 1) % 8 == iota((block * 8, 128), 0) % 8
    row8 = iota((8, panels), 0).astype(F32)

    def build(step, carry):
        base = step * block
        low, high = [], []
        for d in range(block):
            slot = jnp.broadcast_to(rank_scr[pl.ds(base + d, 1), :], (8, panels))
            slot2 = jnp.broadcast_to(rank_scr2[pl.ds(base + d, 1), :], (8, panels))
            for rows, offset in ((low, 0.0), (high, 8.0)):
                rows.append(
                    jnp.concatenate(
                        [
                            jnp.where(slot == row8 + offset, 1.0, 0.0),
                            jnp.where(slot2 == row8 + offset, 1.0, 0.0),
                        ],
                        axis=1,
                    )
                )
        picked = dot(jnp.concatenate(low + high, axis=0).astype(BF16), pay_parts[...])
        front, rear = picked[:, 0:128], picked[:, 128:256]
        front = front + pltpu.roll(front, 64, 1)
        turned = pltpu.roll(rear, 64, 1)
        half = block * 8
        rows = jnp.where(left, front[:half] + rear[:half], front[half:] + turned[half:])
        out_box[pl.ds(base, block), 0:8, :] = rows.reshape(block, 8, 128)
        named_id = jnp.where(left, turned[:half], rear[half:]) + 256.0
        named_id = jnp.where(own_row, named_id, 0.0).reshape(block, 8, 128)
        out_box[pl.ds(base, block), 8, :] = jnp.sum(named_id, axis=1)
        return carry

    lax.fori_loop(0, n // block, build, 0)

    pl.semaphore_wait(barrier, n - 1)

    def send(i, carry):
        p = (me + i) % n
        pltpu.make_async_remote_copy(
            src_ref=out_box.at[p],
            dst_ref=in_box.at[me],
            send_sem=send_sem,
            recv_sem=recv_sem.at[me // 8],
            device_id=device(p),
            device_id_type=MESH,
        ).start()
        return carry

    lax.fori_loop(1, n, send, 0, unroll=True)
    pltpu.make_async_copy(out_box.at[me], in_box.at[me], recv_sem.at[me // 8]).start()

    for load in loads[4:]:
        load.wait()
    home = iota((n, count), 0) == home_ref[...]
    home_rank = jnp.where(home, dot(home.astype(F32).astype(BF16), earlier), -1.0)
    for r in range(8):
        pick_back[n * r : n * (r + 1), :] = jnp.where(home_rank == float(r), 1.0, 0.0).astype(BF16)
    centres = centres_ref[...]
    for row in range(64):
        stage[row * 8 : row * 8 + 3, :] = targets_ref[:, row * 128 : (row + 1) * 128]
    tall = [stage[pl.ds(c, 64, stride=8), :] for c in range(3)]
    blank = jnp.zeros((64, 128), F32)
    tall = [
        jnp.concatenate([tall[0], blank], axis=0).T,
        jnp.concatenate([blank, tall[1]], axis=0).T,
        jnp.concatenate([tall[2], blank], axis=0).T,
    ]
    tall = [part.astype(F32) for triple in zip(*[split3(v) for v in tall]) for part in triple]
    tall = jnp.concatenate(
        [
            jnp.concatenate([v[g * NODES : (g + 1) * NODES, :] for g in range(8)], axis=1)
            for v in tall
        ],
        axis=0,
    ).astype(BF16)
    spread = iota((8 * 128, count), 0)
    spread = (spread % 64) * 8 + spread // 128 == iota((8 * 128, count), 1)
    tall = dot(tall, jnp.where(spread, 1.0, 0.0).astype(BF16))
    tall = tall[0:48, :] + tall[48:96, :] + tall[96:144, :]
    tx = tall[0:16, :] - centres[0:1, :]
    ty = tall[16:32, :] - centres[1:2, :]
    tz = tall[32:48, :] - centres[2:3, :]

    def keep(m, l, part, value):
        table[PLACE[(m, l, part)]] = value * weight(l, m)

    harmonics(tx, ty, tz, tx * tx + ty * ty + tz * tz, jnp.ones_like(tx), keep)
    padded = jnp.concatenate([centres, jnp.zeros((5, count), F32)], axis=0)
    centre_parts = jnp.concatenate(
        [part.astype(F32) for part in split3(padded)] + [jnp.zeros((8, count), F32)], axis=0
    ).astype(BF16)
    lanes = jnp.concatenate([up_ref[...]] * 8, axis=0)
    is_density = (iota(lanes.shape, 0) // NODES) % 4 == 3
    lanes = jnp.where(is_density, lanes * fw_ref[...], lanes)
    lanes = jnp.concatenate([lanes, lanes], axis=1).T[0:FINE, :]
    which = (iota(lanes.shape, 1) // NODES) % 4
    up = jnp.concatenate([jnp.where(which == c, lanes, 0.0) for c in range(4)], axis=0)
    up_hi, up_mid, _ = split3(up)
    up_ref2[...] = jnp.concatenate([up_hi, up_hi, up_mid, up_mid], axis=1)
    local[...] = jnp.zeros_like(local)
    moments_a[...] = jnp.zeros_like(moments_a)
    moments_b[...] = jnp.zeros_like(moments_b)
    pick_b[...] = jnp.zeros_like(pick_b)
    lane64 = iota((64, 128), 1) < 64
    source_row = (iota((8, 128), 1) // 8) % 8 == iota((8, 128), 0)
    index = iota((count, 128), 0).astype(F32)

    def prepare(step, points, pick):
        q = (me // 8 + groups - step) % groups
        pltpu.make_async_copy(
            out_box.at[pl.ds(0, 8)], in_box.at[pl.ds(q * 8, 8)], recv_sem.at[q]
        ).wait()
        rows = in_box[pl.ds(q * 8, 8), 0:8, :].reshape(64, 128)
        rows = jnp.concatenate([jnp.where(lane64, rows, 0.0), jnp.where(lane64, 0.0, rows)], axis=0)
        hi = rows.astype(BF16)
        mid = (rows - hi.astype(F32)).astype(BF16)
        both = jnp.concatenate([hi, mid, hi, mid], axis=1)
        fine = dot(up_ref2[...], both, NT)
        named = in_box[pl.ds(q * 8, 8), 8, :]
        named = jnp.sum(jnp.where(source_row, named, 0.0), axis=0, keepdims=True)
        picked = jnp.where(index == named, 1.0, 0.0).astype(BF16)
        centre = dot(centre_parts, picked)
        centre = centre[0:8, :] + centre[8:16, :] + centre[16:24, :]
        pick[:, 0:128] = picked
        pick[:, 128:256] = picked
        for c in range(3):
            points[c * FINE : (c + 1) * FINE, :] = fine[c * FINE : (c + 1) * FINE, :] - centre[c : c + 1, :]
        points[3 * FINE : 4 * FINE, :] = fine[3 * FINE : 4 * FINE, :]

    def expand(points, moments):
        part_rows = 32
        for piece in range(FINE // part_rows):
            at = piece * part_rows
            x = points[at : at + part_rows, :]
            y = points[FINE + at : FINE + at + part_rows, :]
            z = points[2 * FINE + at : 2 * FINE + at + part_rows, :]
            strength = points[3 * FINE + at : 3 * FINE + at + part_rows, :]
            dist = jnp.maximum(x * x + y * y + z * z, 0.01)
            inverse = 1.0 / dist
            start = strength * jnp.sqrt(inverse)

            def add(m, l, part, value):
                total = value[0:8, :]
                for k in range(1, part_rows // 8):
                    total = total + value[8 * k : 8 * k + 8, :]
                place = PLACE[(m, l, part)] * 8
                if piece:
                    total = total + moments[place : place + 8, :]
                moments[place : place + 8, :] = total

            harmonics(x * inverse, y * inverse, z * inverse, inverse, start, add)

    def gather(moments, pick):
        total = moments[pl.ds(0, ROWS, stride=8), :]
        for k in range(1, 8):
            total = total + moments[pl.ds(k, ROWS, stride=8), :]
        hi = total.astype(BF16).astype(F32)
        both = jnp.concatenate([hi, total - hi], axis=1).astype(BF16)
        local[...] += dot(both, pick[...], NT)

    prepare(0, points_a, pick_a)

    def pair(i, carry):
        gather(moments_b, pick_b)
        prepare(2 * i + 1, points_b, pick_b)
        expand(points_a, moments_a)
        gather(moments_a, pick_a)
        prepare(2 * i + 2, points_a, pick_a)
        expand(points_b, moments_b)
        return carry

    lax.fori_loop(0, groups // 2 - 1, pair, 0)
    gather(moments_b, pick_b)
    prepare(groups - 1, points_b, pick_b)
    expand(points_a, moments_a)
    gather(moments_a, pick_a)
    expand(points_b, moments_b)
    gather(moments_b, pick_b)

    potential = jnp.zeros((NODES, count), F32)
    for place in range(len(PLACE)):
        potential = potential + table[place] * local[place : place + 1, :]
    back = jnp.concatenate([potential] * 8, axis=0)
    back = jnp.concatenate([part.astype(F32) for part in split3(back)], axis=0).astype(BF16)
    lane_slot = iota((n, 128), 1) // NODES
    answer = jnp.zeros((n, 128), F32)
    found = dot(pick_back[...], back, NT)
    found = found[:, 0:128] + found[:, 128:256] + found[:, 256:384]
    for r in range(8):
        answer = jnp.where(lane_slot == r, found[n * r : n * (r + 1), :], answer)
    back_box[...] = answer.reshape(n, 1, 128)

    def send_back(i, carry):
        p = (me + i) % n
        pltpu.make_async_remote_copy(
            src_ref=back_box.at[p],
            dst_ref=out_ref.at[me],
            send_sem=back_send_sem,
            recv_sem=back_recv_sem,
            device_id=device(p),
            device_id_type=MESH,
        ).start()
        return carry

    lax.fori_loop(1, n, send_back, 0, unroll=True)
    pltpu.make_async_copy(back_box.at[me], out_ref.at[me], back_recv_sem).start()
    pltpu.make_async_copy(
        out_box.at[pl.ds(0, n - 1)], in_box.at[pl.ds(0, n - 1)], send_sem
    ).wait()
    pltpu.make_async_copy(
        back_box.at[pl.ds(0, n - 1)], out_ref.at[pl.ds(0, n - 1)], back_send_sem
    ).wait()
    pltpu.make_async_copy(back_box, out_ref, back_recv_sem).wait()


def per_device(
    grp_size,
    dev_size,
    panel_nodes,
    density,
    crevice_routes,
    crevice_centre,
    centres,
    targets,
    centre_home,
    upsample,
    fine_weights,
):
    n = grp_size * dev_size
    panels = crevice_routes.shape[0]
    count = centres.shape[1]
    vmem = pl.BlockSpec(memory_space=pltpu.VMEM)
    returned = pl.pallas_call(
        functools.partial(kernel, grp_size, dev_size),
        out_shape=pltpu.VMEM((n, 1, 128), F32),
        in_specs=[pl.BlockSpec(memory_space=pltpu.HBM)] * 9,
        out_specs=vmem,
        scratch_shapes=[
            pltpu.VMEM((512, 128), F32),
            pltpu.VMEM((panels, 128), F32),
            pltpu.VMEM((2 * panels, 256), BF16),
            pltpu.VMEM((n, panels), F32),
            pltpu.VMEM((n, panels), F32),
            pltpu.VMEM((n, 9, 128), F32),
            pltpu.VMEM((n, 9, 128), F32),
            pltpu.VMEM((n, 1, 128), F32),
            pltpu.VMEM((len(PLACE), NODES, count), F32),
            pltpu.VMEM((8 * n, count), BF16),
            pltpu.VMEM((4 * FINE, 512), BF16),
            pltpu.VMEM((4 * FINE, 128), F32),
            pltpu.VMEM((4 * FINE, 128), F32),
            pltpu.VMEM((count, 256), BF16),
            pltpu.VMEM((count, 256), BF16),
            pltpu.VMEM((ROWS * 8, 128), F32),
            pltpu.VMEM((ROWS * 8, 128), F32),
            pltpu.VMEM((ROWS, count), F32),
            pltpu.SemaphoreType.DMA,
            pltpu.SemaphoreType.DMA((n // 8,)),
            pltpu.SemaphoreType.DMA,
            pltpu.SemaphoreType.DMA,
            pltpu.VMEM((3, panels * NODES), F32),
            pltpu.VMEM((panels * NODES // 128, 128), F32),
            pltpu.VMEM((2, panels), jnp.int32),
            pltpu.VMEM((2, panels), jnp.int32),
            pltpu.VMEM((1, count), jnp.int32),
            pltpu.VMEM((3, count), F32),
            pltpu.VMEM((3, count * NODES), F32),
            pltpu.VMEM((NODES, FINE), F32),
            pltpu.VMEM((1, FINE), F32),
            pltpu.SemaphoreType.DMA((9,)),
        ],
        compiler_params=pltpu.CompilerParams(
            collective_id=0, has_side_effects=True, vmem_limit_bytes=58 << 20
        ),
    )(
        panel_nodes,
        density.reshape(panels * NODES // 128, 128),
        crevice_routes.T,
        crevice_centre.T,
        centre_home.reshape(1, count),
        centres,
        targets,
        upsample.T,
        fine_weights.reshape(1, FINE),
    )
    return returned.reshape(-1)


def solution(mesh):
    split = P(None, ("grp", "dev"))
    rows = P(("grp", "dev"), None)
    placed = (split, P(("grp", "dev")), rows, rows, split, split, rows, P(), P())
    return jax.shard_map(
        functools.partial(per_device, mesh.shape["grp"], mesh.shape["dev"]),
        mesh=mesh,
        in_specs=placed,
        out_specs=P(("grp", "dev")),
        check_vma=False,
    )
```

```python
import functools
import math

import jax
import jax.numpy as jnp
from jax import lax
from jax.experimental import pallas as pl
from jax.experimental.pallas import tpu as pltpu
from jax.sharding import PartitionSpec as P

MESH = pl.DeviceIdType.MESH
F32, BF16 = jnp.float32, jnp.bfloat16
ORDER = 8
NODES = 16
FINE = 64
NN = (((1,), (0,)), ((), ()))
NT = (((1,), (1,)), ((), ()))
TERMS = [(m, l) for m in range(ORDER + 1) for l in range(m, ORDER + 1)]
ROWS = 88


def rows_of():
    at, place = {}, 0
    for m in range(ORDER + 1):
        for l in range(m, ORDER + 1):
            for part in range(1 if m == 0 else 2):
                at[(m, l, part)] = place
                place += 1
    return at


PLACE = rows_of()


def weight(l, m):
    lead = math.factorial(2 * l) / (2**l * math.factorial(l) * math.factorial(l - m))
    return (1 if m == 0 else 2) * math.factorial(l - m) / math.factorial(l + m) * lead * lead


def harmonics(x, y, z, sq, start, emit):
    re, im = start, None
    for m in range(ORDER + 1):
        if m == 1:
            re, im = x * start, y * start
        elif m > 1:
            re, im = x * re - y * im, x * im + y * re
        old_re = old_im = None
        now_re, now_im = re, im
        for l in range(m, ORDER + 1):
            emit(m, l, 0, now_re)
            if m:
                emit(m, l, 1, now_im)
            if l == ORDER:
                break
            next_re = z * now_re
            next_im = z * now_im if m else None
            if l > m:
                damp = sq * ((l * l - m * m) / (4.0 * l * l - 1.0))
                next_re = next_re - damp * old_re
                if m:
                    next_im = next_im - damp * old_im
            old_re, old_im, now_re, now_im = now_re, now_im, next_re, next_im


def split3(value):
    hi = value.astype(BF16)
    rest = value - hi.astype(F32)
    mid = rest.astype(BF16)
    return hi, mid, (rest - mid.astype(F32)).astype(BF16)


def dot(a, b, dims=NN):
    return lax.dot_general(a, b, dims, preferred_element_type=F32)


def iota(shape, axis):
    return lax.broadcasted_iota(jnp.int32, shape, axis)


def kernel(
    grp_size,
    dev_size,
    nodes_hbm,
    density_hbm,
    routes_hbm,
    ids_hbm,
    home_hbm,
    centres_hbm,
    targets_hbm,
    up_hbm,
    fw_hbm,
    out_ref,
    stage,
    pay_scr,
    pay_parts,
    rank_scr,
    rank_scr2,
    out_box,
    in_box,
    back_box,
    table,
    pick_back,
    up_ref2,
    points_a,
    points_b,
    pick_a,
    pick_b,
    moments_a,
    moments_b,
    local,
    send_sem,
    recv_sem,
    back_send_sem,
    back_recv_sem,
    nodes_ref,
    density_ref,
    routes_ref,
    ids_ref,
    home_ref,
    centres_ref,
    targets_ref,
    up_ref,
    fw_ref,
    load_sem,
):
    n = grp_size * dev_size
    loads = [
        pltpu.make_async_copy(source, copy, load_sem.at[i])
        for i, (source, copy) in enumerate(
            (
                (nodes_hbm, nodes_ref),
                (density_hbm, density_ref),
                (routes_hbm, routes_ref),
                (ids_hbm, ids_ref),
                (home_hbm, home_ref),
                (centres_hbm, centres_ref),
                (targets_hbm, targets_ref),
                (up_hbm, up_ref),
                (fw_hbm, fw_ref),
            )
        )
    ]
    for load in loads:
        load.start()
    panels = routes_ref.shape[1]
    count = centres_ref.shape[1]
    groups = n // 8
    me = lax.axis_index("grp") * dev_size + lax.axis_index("dev")

    def device(p):
        return (p // dev_size, p % dev_size)

    barrier = pltpu.get_barrier_semaphore()

    def greet(i, carry):
        pl.semaphore_signal(barrier, inc=1, device_id=device((me + i) % n), device_id_type=MESH)
        return carry

    lax.fori_loop(1, n, greet, 0, unroll=True)
    for load in loads[:4]:
        load.wait()

    lane = iota((64, 128), 1)
    for row in range(64):
        stage[row * 8 : row * 8 + 3, :] = nodes_ref[:, row * 128 : (row + 1) * 128]
    parts_of = [stage[pl.ds(c, 64, stride=8), :] for c in range(3)] + [density_ref[...]]
    turned = [[pltpu.roll(v, t * NODES, 1) if t else v for t in range(8)] for v in parts_of]
    for g in range(8):
        built = turned[0][(0 - g) % 8]
        for c in range(1, 8):
            built = jnp.where(lane // NODES == c, turned[c % 4][(c - g) % 8], built)
        pay_scr[pl.ds(g, 64, stride=8), :] = built
    owner = iota((n, panels), 0)
    first, second = owner == routes_ref[0:1, :], owner == routes_ref[1:2, :]
    named = first | second
    earlier = (iota((panels, panels), 0) < iota((panels, panels), 1)).astype(F32).astype(BF16)
    rank = dot(named.astype(F32).astype(BF16), earlier)
    rank_scr[...] = jnp.where(first, rank, -1.0)
    rank_scr2[...] = jnp.where(second, rank, -1.0)
    ids = ids_ref[...].astype(F32) - 256.0
    for block in range(panels // 128):
        at = block * 128
        square = jnp.concatenate(
            [jnp.broadcast_to(ids[r : r + 1, at : at + 128], (64, 128)) for r in range(2)], axis=0
        ).T
        hi, mid, lo = split3(pay_scr[at : at + 128, :])
        left = iota((128, 128), 1) < 64
        front = jnp.where(left, hi.astype(F32), mid.astype(F32)).astype(BF16)
        low = lo.astype(F32)
        pay_parts[at : at + 128, 0:128] = front
        pay_parts[panels + at : panels + at + 128, 0:128] = front
        pay_parts[at : at + 128, 128:256] = jnp.where(left, low, pltpu.roll(square, 64, 1)).astype(BF16)
        pay_parts[panels + at : panels + at + 128, 128:256] = jnp.where(left, low, square).astype(BF16)
    block = 32
    left = iota((block * 8, 128), 1) < 64
    own_row = iota((block * 8, 128), 1) % 8 == iota((block * 8, 128), 0) % 8
    row8 = iota((8, panels), 0).astype(F32)

    def build(step, carry):
        base = step * block
        low, high = [], []
        for d in range(block):
            slot = jnp.broadcast_to(rank_scr[pl.ds(base + d, 1), :], (8, panels))
            slot2 = jnp.broadcast_to(rank_scr2[pl.ds(base + d, 1), :], (8, panels))
            for rows, offset in ((low, 0.0), (high, 8.0)):
                rows.append(
                    jnp.concatenate(
                        [
                            jnp.where(slot == row8 + offset, 1.0, 0.0),
                            jnp.where(slot2 == row8 + offset, 1.0, 0.0),
                        ],
                        axis=1,
                    )
                )
        picked = dot(jnp.concatenate(low + high, axis=0).astype(BF16), pay_parts[...])
        front, rear = picked[:, 0:128], picked[:, 128:256]
        front = front + pltpu.roll(front, 64, 1)
        turned = pltpu.roll(rear, 64, 1)
        half = block * 8
        rows = jnp.where(left, front[:half] + rear[:half], front[half:] + turned[half:])
        out_box[pl.ds(base, block), 0:8, :] = rows.reshape(block, 8, 128)
        named_id = jnp.where(left, turned[:half], rear[half:]) + 256.0
        named_id = jnp.where(own_row, named_id, 0.0).reshape(block, 8, 128)
        out_box[pl.ds(base, block), 8, :] = jnp.sum(named_id, axis=1)
        return carry

    lax.fori_loop(0, n // block, build, 0)

    pl.semaphore_wait(barrier, n - 1)

    grp, place = lax.axis_index("grp"), lax.axis_index("dev")
    berth = (place % 8) * groups + me // 8
    wide = dev_size // 8

    def peer(i):
        stage, k = i // groups, i % groups
        column = (grp ^ (k // wide)) * dev_size + (place // 8 + k % wide) % wide * 8
        return column + ((place % 8) ^ stage)

    def send(i):
        p = peer(i)
        pltpu.make_async_remote_copy(
            src_ref=out_box.at[p],
            dst_ref=in_box.at[berth],
            send_sem=send_sem,
            recv_sem=recv_sem.at[berth // 8],
            device_id=device(p),
            device_id_type=MESH,
        ).start()

    for i in range(1, n):
        send(i)
    pltpu.make_async_copy(out_box.at[me], in_box.at[berth], recv_sem.at[berth // 8]).start()

    for load in loads[4:]:
        load.wait()
    home = iota((n, count), 0) == home_ref[...]
    home_rank = jnp.where(home, dot(home.astype(F32).astype(BF16), earlier), -1.0)
    for r in range(8):
        pick_back[n * r : n * (r + 1), :] = jnp.where(home_rank == float(r), 1.0, 0.0).astype(BF16)
    centres = centres_ref[...]
    for row in range(64):
        stage[row * 8 : row * 8 + 3, :] = targets_ref[:, row * 128 : (row + 1) * 128]
    tall = [stage[pl.ds(c, 64, stride=8), :] for c in range(3)]
    blank = jnp.zeros((64, 128), F32)
    tall = [
        jnp.concatenate([tall[0], blank], axis=0).T,
        jnp.concatenate([blank, tall[1]], axis=0).T,
        jnp.concatenate([tall[2], blank], axis=0).T,
    ]
    tall = [part.astype(F32) for triple in zip(*[split3(v) for v in tall]) for part in triple]
    tall = jnp.concatenate(
        [
            jnp.concatenate([v[g * NODES : (g + 1) * NODES, :] for g in range(8)], axis=1)
            for v in tall
        ],
        axis=0,
    ).astype(BF16)
    spread = iota((8 * 128, count), 0)
    spread = (spread % 64) * 8 + spread // 128 == iota((8 * 128, count), 1)
    tall = dot(tall, jnp.where(spread, 1.0, 0.0).astype(BF16))
    tall = tall[0:48, :] + tall[48:96, :] + tall[96:144, :]
    tx = tall[0:16, :] - centres[0:1, :]
    ty = tall[16:32, :] - centres[1:2, :]
    tz = tall[32:48, :] - centres[2:3, :]

    def keep(m, l, part, value):
        table[PLACE[(m, l, part)]] = value * weight(l, m)

    harmonics(tx, ty, tz, tx * tx + ty * ty + tz * tz, jnp.ones_like(tx), keep)
    padded = jnp.concatenate([centres, jnp.zeros((5, count), F32)], axis=0)
    centre_parts = jnp.concatenate(
        [part.astype(F32) for part in split3(padded)] + [jnp.zeros((8, count), F32)], axis=0
    ).astype(BF16)
    lanes = jnp.concatenate([up_ref[...]] * 8, axis=0)
    is_density = (iota(lanes.shape, 0) // NODES) % 4 == 3
    lanes = jnp.where(is_density, lanes * fw_ref[...], lanes)
    lanes = jnp.concatenate([lanes, lanes], axis=1).T[0:FINE, :]
    which = (iota(lanes.shape, 1) // NODES) % 4
    up = jnp.concatenate([jnp.where(which == c, lanes, 0.0) for c in range(4)], axis=0)
    up_hi, up_mid, _ = split3(up)
    up_ref2[...] = jnp.concatenate([up_hi, up_hi, up_mid, up_mid], axis=1)
    local[...] = jnp.zeros_like(local)
    moments_a[...] = jnp.zeros_like(moments_a)
    moments_b[...] = jnp.zeros_like(moments_b)
    pick_b[...] = jnp.zeros_like(pick_b)
    lane64 = iota((64, 128), 1) < 64
    source_row = (iota((8, 128), 1) // 8) % 8 == iota((8, 128), 0)
    index = iota((count, 128), 0).astype(F32)

    def prepare(step, points, pick):
        q = ((place % 8) ^ (step // 2)) * 2 + ((grp // (grp_size // 2)) ^ (step % 2))
        pltpu.make_async_copy(
            out_box.at[pl.ds(0, 8)], in_box.at[pl.ds(q * 8, 8)], recv_sem.at[q]
        ).wait()
        rows = in_box[pl.ds(q * 8, 8), 0:8, :].reshape(64, 128)
        rows = jnp.concatenate([jnp.where(lane64, rows, 0.0), jnp.where(lane64, 0.0, rows)], axis=0)
        hi = rows.astype(BF16)
        mid = (rows - hi.astype(F32)).astype(BF16)
        both = jnp.concatenate([hi, mid, hi, mid], axis=1)
        fine = dot(up_ref2[...], both, NT)
        named = in_box[pl.ds(q * 8, 8), 8, :]
        named = jnp.sum(jnp.where(source_row, named, 0.0), axis=0, keepdims=True)
        picked = jnp.where(index == named, 1.0, 0.0).astype(BF16)
        centre = dot(centre_parts, picked)
        centre = centre[0:8, :] + centre[8:16, :] + centre[16:24, :]
        pick[:, 0:128] = picked
        pick[:, 128:256] = picked
        for c in range(3):
            points[c * FINE : (c + 1) * FINE, :] = fine[c * FINE : (c + 1) * FINE, :] - centre[c : c + 1, :]
        points[3 * FINE : 4 * FINE, :] = fine[3 * FINE : 4 * FINE, :]

    def expand(points, moments):
        part_rows = 32
        for piece in range(FINE // part_rows):
            at = piece * part_rows
            x = points[at : at + part_rows, :]
            y = points[FINE + at : FINE + at + part_rows, :]
            z = points[2 * FINE + at : 2 * FINE + at + part_rows, :]
            strength = points[3 * FINE + at : 3 * FINE + at + part_rows, :]
            dist = jnp.maximum(x * x + y * y + z * z, 0.01)
            inverse = 1.0 / dist
            start = strength * jnp.sqrt(inverse)

            def add(m, l, part, value):
                total = value[0:8, :]
                for k in range(1, part_rows // 8):
                    total = total + value[8 * k : 8 * k + 8, :]
                place = PLACE[(m, l, part)] * 8
                if piece:
                    total = total + moments[place : place + 8, :]
                moments[place : place + 8, :] = total

            harmonics(x * inverse, y * inverse, z * inverse, inverse, start, add)

    def gather(moments, pick):
        total = moments[pl.ds(0, ROWS, stride=8), :]
        for k in range(1, 8):
            total = total + moments[pl.ds(k, ROWS, stride=8), :]
        hi = total.astype(BF16).astype(F32)
        both = jnp.concatenate([hi, total - hi], axis=1).astype(BF16)
        local[...] += dot(both, pick[...], NT)

    prepare(0, points_a, pick_a)

    def pair(i, carry):
        gather(moments_b, pick_b)
        prepare(2 * i + 1, points_b, pick_b)
        expand(points_a, moments_a)
        gather(moments_a, pick_a)
        prepare(2 * i + 2, points_a, pick_a)
        expand(points_b, moments_b)
        return carry

    lax.fori_loop(0, groups // 2 - 1, pair, 0)
    gather(moments_b, pick_b)
    prepare(groups - 1, points_b, pick_b)
    expand(points_a, moments_a)
    gather(moments_a, pick_a)
    expand(points_b, moments_b)
    gather(moments_b, pick_b)

    potential = jnp.zeros((NODES, count), F32)
    for place in range(len(PLACE)):
        potential = potential + table[place] * local[place : place + 1, :]
    back = jnp.concatenate([potential] * 8, axis=0)
    back = jnp.concatenate([part.astype(F32) for part in split3(back)], axis=0).astype(BF16)
    lane_slot = iota((n, 128), 1) // NODES
    answer = jnp.zeros((n, 128), F32)
    found = dot(pick_back[...], back, NT)
    found = found[:, 0:128] + found[:, 128:256] + found[:, 256:384]
    for r in range(8):
        answer = jnp.where(lane_slot == r, found[n * r : n * (r + 1), :], answer)
    back_box[...] = answer.reshape(n, 1, 128)

    def send_back(i, carry):
        p = (me + i) % n
        pltpu.make_async_remote_copy(
            src_ref=back_box.at[p],
            dst_ref=out_ref.at[me],
            send_sem=back_send_sem,
            recv_sem=back_recv_sem,
            device_id=device(p),
            device_id_type=MESH,
        ).start()
        return carry

    lax.fori_loop(1, n, send_back, 0, unroll=True)
    pltpu.make_async_copy(back_box.at[me], out_ref.at[me], back_recv_sem).start()
    pltpu.make_async_copy(
        out_box.at[pl.ds(0, n - 1)], in_box.at[pl.ds(0, n - 1)], send_sem
    ).wait()
    pltpu.make_async_copy(
        back_box.at[pl.ds(0, n - 1)], out_ref.at[pl.ds(0, n - 1)], back_send_sem
    ).wait()
    pltpu.make_async_copy(back_box, out_ref, back_recv_sem).wait()


def per_device(
    grp_size,
    dev_size,
    panel_nodes,
    density,
    crevice_routes,
    crevice_centre,
    centres,
    targets,
    centre_home,
    upsample,
    fine_weights,
):
    n = grp_size * dev_size
    panels = crevice_routes.shape[0]
    count = centres.shape[1]
    vmem = pl.BlockSpec(memory_space=pltpu.VMEM)
    returned = pl.pallas_call(
        functools.partial(kernel, grp_size, dev_size),
        out_shape=pltpu.VMEM((n, 1, 128), F32),
        in_specs=[pl.BlockSpec(memory_space=pltpu.HBM)] * 9,
        out_specs=vmem,
        scratch_shapes=[
            pltpu.VMEM((512, 128), F32),
            pltpu.VMEM((panels, 128), F32),
            pltpu.VMEM((2 * panels, 256), BF16),
            pltpu.VMEM((n, panels), F32),
            pltpu.VMEM((n, panels), F32),
            pltpu.VMEM((n, 9, 128), F32),
            pltpu.VMEM((n, 9, 128), F32),
            pltpu.VMEM((n, 1, 128), F32),
            pltpu.VMEM((len(PLACE), NODES, count), F32),
            pltpu.VMEM((8 * n, count), BF16),
            pltpu.VMEM((4 * FINE, 512), BF16),
            pltpu.VMEM((4 * FINE, 128), F32),
            pltpu.VMEM((4 * FINE, 128), F32),
            pltpu.VMEM((count, 256), BF16),
            pltpu.VMEM((count, 256), BF16),
            pltpu.VMEM((ROWS * 8, 128), F32),
            pltpu.VMEM((ROWS * 8, 128), F32),
            pltpu.VMEM((ROWS, count), F32),
            pltpu.SemaphoreType.DMA,
            pltpu.SemaphoreType.DMA((n // 8,)),
            pltpu.SemaphoreType.DMA,
            pltpu.SemaphoreType.DMA,
            pltpu.VMEM((3, panels * NODES), F32),
            pltpu.VMEM((panels * NODES // 128, 128), F32),
            pltpu.VMEM((2, panels), jnp.int32),
            pltpu.VMEM((2, panels), jnp.int32),
            pltpu.VMEM((1, count), jnp.int32),
            pltpu.VMEM((3, count), F32),
            pltpu.VMEM((3, count * NODES), F32),
            pltpu.VMEM((NODES, FINE), F32),
            pltpu.VMEM((1, FINE), F32),
            pltpu.SemaphoreType.DMA((9,)),
        ],
        compiler_params=pltpu.CompilerParams(
            collective_id=0, has_side_effects=True, vmem_limit_bytes=58 << 20
        ),
    )(
        panel_nodes,
        density.reshape(panels * NODES // 128, 128),
        crevice_routes.T,
        crevice_centre.T,
        centre_home.reshape(1, count),
        centres,
        targets,
        upsample.T,
        fine_weights.reshape(1, FINE),
    )
    return returned.reshape(-1)


def solution(mesh):
    split = P(None, ("grp", "dev"))
    rows = P(("grp", "dev"), None)
    placed = (split, P(("grp", "dev")), rows, rows, split, split, rows, P(), P())
    return jax.shard_map(
        functools.partial(per_device, mesh.shape["grp"], mesh.shape["dev"]),
        mesh=mesh,
        in_specs=placed,
        out_specs=P(("grp", "dev")),
        check_vma=False,
    )
```

```python
import functools
import math

import jax
import jax.numpy as jnp
from jax import lax
from jax.experimental import pallas as pl
from jax.experimental.pallas import tpu as pltpu
from jax.sharding import PartitionSpec as P

MESH = pl.DeviceIdType.MESH
F32, BF16 = jnp.float32, jnp.bfloat16
ORDER = 8
NODES = 16
FINE = 64
NN = (((1,), (0,)), ((), ()))
NT = (((1,), (1,)), ((), ()))
TERMS = [(m, l) for m in range(ORDER + 1) for l in range(m, ORDER + 1)]
ROWS = 88


def rows_of():
    at, place = {}, 0
    for m in range(ORDER + 1):
        for l in range(m, ORDER + 1):
            for part in range(1 if m == 0 else 2):
                at[(m, l, part)] = place
                place += 1
    return at


PLACE = rows_of()


def weight(l, m):
    lead = math.factorial(2 * l) / (2**l * math.factorial(l) * math.factorial(l - m))
    return (1 if m == 0 else 2) * math.factorial(l - m) / math.factorial(l + m) * lead * lead


def harmonics(x, y, z, sq, start, emit):
    re, im = start, None
    for m in range(ORDER + 1):
        if m == 1:
            re, im = x * start, y * start
        elif m > 1:
            re, im = x * re - y * im, x * im + y * re
        old_re = old_im = None
        now_re, now_im = re, im
        for l in range(m, ORDER + 1):
            emit(m, l, 0, now_re)
            if m:
                emit(m, l, 1, now_im)
            if l == ORDER:
                break
            next_re = z * now_re
            next_im = z * now_im if m else None
            if l > m:
                damp = sq * ((l * l - m * m) / (4.0 * l * l - 1.0))
                next_re = next_re - damp * old_re
                if m:
                    next_im = next_im - damp * old_im
            old_re, old_im, now_re, now_im = now_re, now_im, next_re, next_im


def split3(value):
    hi = value.astype(BF16)
    rest = value - hi.astype(F32)
    mid = rest.astype(BF16)
    return hi, mid, (rest - mid.astype(F32)).astype(BF16)


def dot(a, b, dims=NN):
    return lax.dot_general(a, b, dims, preferred_element_type=F32)


def iota(shape, axis):
    return lax.broadcasted_iota(jnp.int32, shape, axis)


def kernel(
    grp_size,
    dev_size,
    nodes_hbm,
    density_hbm,
    routes_hbm,
    ids_hbm,
    home_hbm,
    centres_hbm,
    targets_hbm,
    up_hbm,
    fw_hbm,
    out_ref,
    stage,
    pay_scr,
    pay_parts,
    rank_scr,
    rank_scr2,
    out_box,
    in_box,
    back_box,
    table,
    pick_back,
    up_ref2,
    points_a,
    points_b,
    pick_a,
    pick_b,
    moments_a,
    moments_b,
    local,
    send_sem,
    recv_sem,
    back_send_sem,
    back_recv_sem,
    nodes_ref,
    density_ref,
    routes_ref,
    ids_ref,
    home_ref,
    centres_ref,
    targets_ref,
    up_ref,
    fw_ref,
    load_sem,
):
    n = grp_size * dev_size
    loads = [
        pltpu.make_async_copy(source, copy, load_sem.at[i])
        for i, (source, copy) in enumerate(
            (
                (nodes_hbm, nodes_ref),
                (density_hbm, density_ref),
                (routes_hbm, routes_ref),
                (ids_hbm, ids_ref),
                (home_hbm, home_ref),
                (centres_hbm, centres_ref),
                (targets_hbm, targets_ref),
                (up_hbm, up_ref),
                (fw_hbm, fw_ref),
            )
        )
    ]
    for load in loads:
        load.start()
    panels = routes_ref.shape[1]
    count = centres_ref.shape[1]
    groups = n // 8
    me = lax.axis_index("grp") * dev_size + lax.axis_index("dev")

    def device(p):
        return (p // dev_size, p % dev_size)

    barrier = pltpu.get_barrier_semaphore()

    def greet(i, carry):
        pl.semaphore_signal(barrier, inc=1, device_id=device((me + i) % n), device_id_type=MESH)
        return carry

    lax.fori_loop(1, n, greet, 0, unroll=True)
    for load in loads[:4]:
        load.wait()

    lane = iota((64, 128), 1)
    for row in range(64):
        stage[row * 8 : row * 8 + 3, :] = nodes_ref[:, row * 128 : (row + 1) * 128]
    parts_of = [stage[pl.ds(c, 64, stride=8), :] for c in range(3)] + [density_ref[...]]
    turned = [[pltpu.roll(v, t * NODES, 1) if t else v for t in range(8)] for v in parts_of]
    for g in range(8):
        built = turned[0][(0 - g) % 8]
        for c in range(1, 8):
            built = jnp.where(lane // NODES == c, turned[c % 4][(c - g) % 8], built)
        pay_scr[pl.ds(g, 64, stride=8), :] = built
    owner = iota((n, panels), 0)
    first, second = owner == routes_ref[0:1, :], owner == routes_ref[1:2, :]
    named = first | second
    earlier = (iota((panels, panels), 0) < iota((panels, panels), 1)).astype(F32).astype(BF16)
    rank = dot(named.astype(F32).astype(BF16), earlier)
    rank_scr[...] = jnp.where(first, rank, -1.0)
    rank_scr2[...] = jnp.where(second, rank, -1.0)
    ids = ids_ref[...].astype(F32) - 256.0
    for block in range(panels // 128):
        at = block * 128
        square = jnp.concatenate(
            [jnp.broadcast_to(ids[r : r + 1, at : at + 128], (64, 128)) for r in range(2)], axis=0
        ).T
        hi, mid, lo = split3(pay_scr[at : at + 128, :])
        left = iota((128, 128), 1) < 64
        front = jnp.where(left, hi.astype(F32), mid.astype(F32)).astype(BF16)
        low = lo.astype(F32)
        pay_parts[at : at + 128, 0:128] = front
        pay_parts[panels + at : panels + at + 128, 0:128] = front
        pay_parts[at : at + 128, 128:256] = jnp.where(left, low, pltpu.roll(square, 64, 1)).astype(BF16)
        pay_parts[panels + at : panels + at + 128, 128:256] = jnp.where(left, low, square).astype(BF16)
    block = 32
    left = iota((block * 8, 128), 1) < 64
    own_row = iota((block * 8, 128), 1) % 8 == iota((block * 8, 128), 0) % 8
    row8 = iota((8, panels), 0).astype(F32)

    def build(step, carry):
        base = step * block
        low, high = [], []
        for d in range(block):
            slot = jnp.broadcast_to(rank_scr[pl.ds(base + d, 1), :], (8, panels))
            slot2 = jnp.broadcast_to(rank_scr2[pl.ds(base + d, 1), :], (8, panels))
            for rows, offset in ((low, 0.0), (high, 8.0)):
                rows.append(
                    jnp.concatenate(
                        [
                            jnp.where(slot == row8 + offset, 1.0, 0.0),
                            jnp.where(slot2 == row8 + offset, 1.0, 0.0),
                        ],
                        axis=1,
                    )
                )
        picked = dot(jnp.concatenate(low + high, axis=0).astype(BF16), pay_parts[...])
        front, rear = picked[:, 0:128], picked[:, 128:256]
        front = front + pltpu.roll(front, 64, 1)
        turned = pltpu.roll(rear, 64, 1)
        half = block * 8
        rows = jnp.where(left, front[:half] + rear[:half], front[half:] + turned[half:])
        out_box[pl.ds(base, block), 0:8, :] = rows.reshape(block, 8, 128)
        named_id = jnp.where(left, turned[:half], rear[half:]) + 256.0
        named_id = jnp.where(own_row, named_id, 0.0).reshape(block, 8, 128)
        out_box[pl.ds(base, block), 8, :] = jnp.sum(named_id, axis=1)
        return carry

    lax.fori_loop(0, n // block, build, 0, unroll=2)

    pl.semaphore_wait(barrier, n - 1)

    grp, place = lax.axis_index("grp"), lax.axis_index("dev")
    berth = (place % 8) * groups + me // 8
    wide = dev_size // 8

    def peer(i):
        stage, k = i // groups, i % groups
        column = (grp ^ (k // wide)) * dev_size + (place // 8 + k % wide) % wide * 8
        return column + ((place % 8) ^ stage)

    def send(i):
        p = peer(i)
        pltpu.make_async_remote_copy(
            src_ref=out_box.at[p],
            dst_ref=in_box.at[berth],
            send_sem=send_sem,
            recv_sem=recv_sem.at[berth // 8],
            device_id=device(p),
            device_id_type=MESH,
        ).start()

    for i in range(1, n):
        send(i)
    pltpu.make_async_copy(out_box.at[me], in_box.at[berth], recv_sem.at[berth // 8]).start()

    for load in loads[4:]:
        load.wait()
    home = iota((n, count), 0) == home_ref[...]
    home_rank = jnp.where(home, dot(home.astype(F32).astype(BF16), earlier), -1.0)
    for r in range(8):
        pick_back[n * r : n * (r + 1), :] = jnp.where(home_rank == float(r), 1.0, 0.0).astype(BF16)
    centres = centres_ref[...]
    for row in range(64):
        stage[row * 8 : row * 8 + 3, :] = targets_ref[:, row * 128 : (row + 1) * 128]
    tall = [stage[pl.ds(c, 64, stride=8), :] for c in range(3)]
    blank = jnp.zeros((64, 128), F32)
    tall = [
        jnp.concatenate([tall[0], blank], axis=0).T,
        jnp.concatenate([blank, tall[1]], axis=0).T,
        jnp.concatenate([tall[2], blank], axis=0).T,
    ]
    tall = [part.astype(F32) for triple in zip(*[split3(v) for v in tall]) for part in triple]
    tall = jnp.concatenate(
        [
            jnp.concatenate([v[g * NODES : (g + 1) * NODES, :] for g in range(8)], axis=1)
            for v in tall
        ],
        axis=0,
    ).astype(BF16)
    spread = iota((8 * 128, count), 0)
    spread = (spread % 64) * 8 + spread // 128 == iota((8 * 128, count), 1)
    tall = dot(tall, jnp.where(spread, 1.0, 0.0).astype(BF16))
    tall = tall[0:48, :] + tall[48:96, :] + tall[96:144, :]
    tx = tall[0:16, :] - centres[0:1, :]
    ty = tall[16:32, :] - centres[1:2, :]
    tz = tall[32:48, :] - centres[2:3, :]

    def keep(m, l, part, value):
        table[PLACE[(m, l, part)]] = value * weight(l, m)

    harmonics(tx, ty, tz, tx * tx + ty * ty + tz * tz, jnp.ones_like(tx), keep)
    padded = jnp.concatenate([centres, jnp.zeros((5, count), F32)], axis=0)
    centre_parts = jnp.concatenate(
        [part.astype(F32) for part in split3(padded)] + [jnp.zeros((8, count), F32)], axis=0
    ).astype(BF16)
    lanes = jnp.concatenate([up_ref[...]] * 8, axis=0)
    is_density = (iota(lanes.shape, 0) // NODES) % 4 == 3
    lanes = jnp.where(is_density, lanes * fw_ref[...], lanes)
    lanes = jnp.concatenate([lanes, lanes], axis=1).T[0:FINE, :]
    which = (iota(lanes.shape, 1) // NODES) % 4
    up = jnp.concatenate([jnp.where(which == c, lanes, 0.0) for c in range(4)], axis=0)
    up_hi, up_mid, _ = split3(up)
    up_ref2[...] = jnp.concatenate([up_hi, up_hi, up_mid, up_mid], axis=1)
    local[...] = jnp.zeros_like(local)
    moments_a[...] = jnp.zeros_like(moments_a)
    moments_b[...] = jnp.zeros_like(moments_b)
    pick_b[...] = jnp.zeros_like(pick_b)
    lane64 = iota((64, 128), 1) < 64
    source_row = (iota((8, 128), 1) // 8) % 8 == iota((8, 128), 0)
    index = iota((count, 128), 0).astype(F32)

    def prepare(step, points, pick):
        q = ((place % 8) ^ (step // 2)) * 2 + ((grp // (grp_size // 2)) ^ (step % 2))
        pltpu.make_async_copy(
            out_box.at[pl.ds(0, 8)], in_box.at[pl.ds(q * 8, 8)], recv_sem.at[q]
        ).wait()
        rows = in_box[pl.ds(q * 8, 8), 0:8, :].reshape(64, 128)
        rows = jnp.concatenate([jnp.where(lane64, rows, 0.0), jnp.where(lane64, 0.0, rows)], axis=0)
        hi = rows.astype(BF16)
        mid = (rows - hi.astype(F32)).astype(BF16)
        both = jnp.concatenate([hi, mid, hi, mid], axis=1)
        fine = dot(up_ref2[...], both, NT)
        named = in_box[pl.ds(q * 8, 8), 8, :]
        named = jnp.sum(jnp.where(source_row, named, 0.0), axis=0, keepdims=True)
        picked = jnp.where(index == named, 1.0, 0.0).astype(BF16)
        centre = dot(centre_parts, picked)
        centre = centre[0:8, :] + centre[8:16, :] + centre[16:24, :]
        pick[:, 0:128] = picked
        pick[:, 128:256] = picked
        for c in range(3):
            points[c * FINE : (c + 1) * FINE, :] = fine[c * FINE : (c + 1) * FINE, :] - centre[c : c + 1, :]
        points[3 * FINE : 4 * FINE, :] = fine[3 * FINE : 4 * FINE, :]

    def expand(points, moments):
        part_rows = 32
        for piece in range(FINE // part_rows):
            at = piece * part_rows
            x = points[at : at + part_rows, :]
            y = points[FINE + at : FINE + at + part_rows, :]
            z = points[2 * FINE + at : 2 * FINE + at + part_rows, :]
            strength = points[3 * FINE + at : 3 * FINE + at + part_rows, :]
            dist = jnp.maximum(x * x + y * y + z * z, 0.01)
            inverse = 1.0 / dist
            start = strength * jnp.sqrt(inverse)

            def add(m, l, part, value):
                total = value[0:8, :]
                for k in range(1, part_rows // 8):
                    total = total + value[8 * k : 8 * k + 8, :]
                place = PLACE[(m, l, part)] * 8
                if piece:
                    total = total + moments[place : place + 8, :]
                moments[place : place + 8, :] = total

            harmonics(x * inverse, y * inverse, z * inverse, inverse, start, add)

    def gather(moments, pick):
        total = moments[pl.ds(0, ROWS, stride=8), :]
        for k in range(1, 8):
            total = total + moments[pl.ds(k, ROWS, stride=8), :]
        hi = total.astype(BF16).astype(F32)
        both = jnp.concatenate([hi, total - hi], axis=1).astype(BF16)
        local[...] += dot(both, pick[...], NT)

    prepare(0, points_a, pick_a)

    def pair(i, carry):
        gather(moments_b, pick_b)
        prepare(2 * i + 1, points_b, pick_b)
        expand(points_a, moments_a)
        gather(moments_a, pick_a)
        prepare(2 * i + 2, points_a, pick_a)
        expand(points_b, moments_b)
        return carry

    lax.fori_loop(0, groups // 2 - 1, pair, 0)
    gather(moments_b, pick_b)
    prepare(groups - 1, points_b, pick_b)
    expand(points_a, moments_a)
    gather(moments_a, pick_a)
    expand(points_b, moments_b)
    gather(moments_b, pick_b)

    potential = jnp.zeros((NODES, count), F32)
    for place in range(len(PLACE)):
        potential = potential + table[place] * local[place : place + 1, :]
    back = jnp.concatenate([potential] * 8, axis=0)
    back = jnp.concatenate([part.astype(F32) for part in split3(back)], axis=0).astype(BF16)
    lane_slot = iota((n, 128), 1) // NODES
    answer = jnp.zeros((n, 128), F32)
    found = dot(pick_back[...], back, NT)
    found = found[:, 0:128] + found[:, 128:256] + found[:, 256:384]
    for r in range(8):
        answer = jnp.where(lane_slot == r, found[n * r : n * (r + 1), :], answer)
    back_box[...] = answer.reshape(n, 1, 128)

    def send_back(i, carry):
        p = (me + i) % n
        pltpu.make_async_remote_copy(
            src_ref=back_box.at[p],
            dst_ref=out_ref.at[me],
            send_sem=back_send_sem,
            recv_sem=back_recv_sem,
            device_id=device(p),
            device_id_type=MESH,
        ).start()
        return carry

    lax.fori_loop(1, n, send_back, 0, unroll=True)
    pltpu.make_async_copy(back_box.at[me], out_ref.at[me], back_recv_sem).start()
    pltpu.make_async_copy(
        out_box.at[pl.ds(0, n - 1)], in_box.at[pl.ds(0, n - 1)], send_sem
    ).wait()
    pltpu.make_async_copy(
        back_box.at[pl.ds(0, n - 1)], out_ref.at[pl.ds(0, n - 1)], back_send_sem
    ).wait()
    pltpu.make_async_copy(back_box, out_ref, back_recv_sem).wait()


def per_device(
    grp_size,
    dev_size,
    panel_nodes,
    density,
    crevice_routes,
    crevice_centre,
    centres,
    targets,
    centre_home,
    upsample,
    fine_weights,
):
    n = grp_size * dev_size
    panels = crevice_routes.shape[0]
    count = centres.shape[1]
    vmem = pl.BlockSpec(memory_space=pltpu.VMEM)
    returned = pl.pallas_call(
        functools.partial(kernel, grp_size, dev_size),
        out_shape=pltpu.VMEM((n, 1, 128), F32),
        in_specs=[pl.BlockSpec(memory_space=pltpu.HBM)] * 9,
        out_specs=vmem,
        scratch_shapes=[
            pltpu.VMEM((512, 128), F32),
            pltpu.VMEM((panels, 128), F32),
            pltpu.VMEM((2 * panels, 256), BF16),
            pltpu.VMEM((n, panels), F32),
            pltpu.VMEM((n, panels), F32),
            pltpu.VMEM((n, 9, 128), F32),
            pltpu.VMEM((n, 9, 128), F32),
            pltpu.VMEM((n, 1, 128), F32),
            pltpu.VMEM((len(PLACE), NODES, count), F32),
            pltpu.VMEM((8 * n, count), BF16),
            pltpu.VMEM((4 * FINE, 512), BF16),
            pltpu.VMEM((4 * FINE, 128), F32),
            pltpu.VMEM((4 * FINE, 128), F32),
            pltpu.VMEM((count, 256), BF16),
            pltpu.VMEM((count, 256), BF16),
            pltpu.VMEM((ROWS * 8, 128), F32),
            pltpu.VMEM((ROWS * 8, 128), F32),
            pltpu.VMEM((ROWS, count), F32),
            pltpu.SemaphoreType.DMA,
            pltpu.SemaphoreType.DMA((n // 8,)),
            pltpu.SemaphoreType.DMA,
            pltpu.SemaphoreType.DMA,
            pltpu.VMEM((3, panels * NODES), F32),
            pltpu.VMEM((panels * NODES // 128, 128), F32),
            pltpu.VMEM((2, panels), jnp.int32),
            pltpu.VMEM((2, panels), jnp.int32),
            pltpu.VMEM((1, count), jnp.int32),
            pltpu.VMEM((3, count), F32),
            pltpu.VMEM((3, count * NODES), F32),
            pltpu.VMEM((NODES, FINE), F32),
            pltpu.VMEM((1, FINE), F32),
            pltpu.SemaphoreType.DMA((9,)),
        ],
        compiler_params=pltpu.CompilerParams(
            collective_id=0, has_side_effects=True, vmem_limit_bytes=58 << 20
        ),
    )(
        panel_nodes,
        density.reshape(panels * NODES // 128, 128),
        crevice_routes.T,
        crevice_centre.T,
        centre_home.reshape(1, count),
        centres,
        targets,
        upsample.T,
        fine_weights.reshape(1, FINE),
    )
    return returned.reshape(-1)


def solution(mesh):
    split = P(None, ("grp", "dev"))
    rows = P(("grp", "dev"), None)
    placed = (split, P(("grp", "dev")), rows, rows, split, split, rows, P(), P())
    return jax.shard_map(
        functools.partial(per_device, mesh.shape["grp"], mesh.shape["dev"]),
        mesh=mesh,
        in_specs=placed,
        out_specs=P(("grp", "dev")),
        check_vma=False,
    )
```
